256 devices in a mesh: seq: 8 (over x, core), head: 32 (over y, z).
Axes of the slice: x: 4, y: 4, z: 8, core: 2. Of those that a mesh axis runs over, the one named last changes fastest.
Arguments:
- inputs: bfloat16 [81920, 8192], P(('seq', 'head')), may hold values from -6 to 6
- b_panel: bfloat16 [81920, 128], P(('seq', 'head')), may hold values from -0.52734375 to 0.52734375
- c_panel: bfloat16 [81920, 128], P(('seq', 'head')), may hold values from -0.52734375 to 0.52734375
- dt_raw: bfloat16 [81920, 128], P(('seq', 'head')), may hold values from -3 to 3
- dt_bias: float32 [128], replicated, may hold values from -3.5 to 0.5
- a_log: float32 [128], replicated, may hold values from -12 to 1
- d_skip: float32 [128], replicated, may hold values from 0.5 to 1.5
Outputs:
- mixed: bfloat16 [81920, 8192], P(('seq', 'head'))
The draws below stay inside these ranges and needn't reach their ends.
All inputs are finite; a program needn't handle non-finite values.
Results may differ from the reference program's by a relative error of at most 0.0051.
Values may be sent and summed in bfloat16 or wider, within the bound.
A program may use at most 128 MiB of HBM per device.

```python
import jax
import jax.numpy as jnp
from jax import lax

HEADS = 128
HDIM = 64
DSTATE = 128
SPAN = 256
SEQ_LEN = 81920


def rate_table(key):
    key_order = jax.random.fold_in(key, 11)
    key_bias = jax.random.fold_in(key, 12)
    key_reach = jax.random.fold_in(key, 13)
    key_memory = jax.random.fold_in(key, 14)
    order = jax.random.permutation(key_order, HEADS)
    slow = order < HEADS // 2
    slow_bias = jax.random.uniform(key_bias, (HEADS,), jnp.float32, -3.5, -2.5)
    fast_bias = slow_bias + 3.0
    bias = jnp.where(slow, slow_bias, fast_bias)
    nominal = jax.nn.softplus(bias)
    reach = jax.random.uniform(key_reach, (HEADS,), jnp.float32, 0.5, 1.5)
    memory = jax.random.uniform(key_memory, (HEADS,), jnp.float32, 0.12, 0.2) * SPAN
    rate = jnp.where(slow, reach / (SEQ_LEN * nominal), 1.0 / (memory * nominal))
    return (bias, jnp.log(rate))


def draw_dt_bias(key, part):
    return rate_table(key)[0]


def draw_a_log(key, part):
    return rate_table(key)[1]


def shard_levels(key, dims, split, smallest, top_value):
    factor_of = 1.0
    for axis_at, parts in split:
        steps = jax.random.uniform(jax.random.fold_in(jax.random.fold_in(key, 6), axis_at), (parts,), jnp.float32, smallest / len(split), top_value / len(split))
        factor_of = factor_of * jnp.repeat(jnp.exp(steps), dims[axis_at] // parts).reshape((-1,) + (1,) * (len(dims) - 1 - axis_at))
    return factor_of


def scatter_about(own_key, shape, scale, bound, cuts=(), kind=jnp.bfloat16):
    array = jax.random.normal(own_key, shape, jnp.float32) * scale
    if len(cuts) > 0:
        array = shard_levels(own_key, shape, cuts, -0.22, 0.18) * array
    return jnp.clip(array, min=-bound, max=bound).astype(kind)


def setup_inputs(seed: int = 0) -> dict:
    key_list = jax.random.split(jax.random.key(seed), 8)
    return {
        "inputs": scatter_about(key_list[0], (SEQ_LEN, HEADS * HDIM), 1.0, 6.0, ((0, 256),)),
        "b_panel": scatter_about(key_list[1], (SEQ_LEN, DSTATE), (DSTATE ** -0.5), 0.52734375, ((0, 256),)),
        "c_panel": scatter_about(key_list[2], (SEQ_LEN, DSTATE), (DSTATE ** -0.5), 0.52734375, ((0, 256),)),
        "dt_raw": scatter_about(key_list[3], (SEQ_LEN, HEADS), 0.5, 3.0, ((0, 256),)),
        "dt_bias": draw_dt_bias(jax.random.fold_in(key_list[7], 71), 0),
        "a_log": draw_a_log(jax.random.fold_in(key_list[7], 71), 0),
        "d_skip": jnp.clip(jax.random.uniform(key_list[6], (HEADS,), jnp.float32, 0.5, 1.5), 0.5, 1.5),
    }


def span_terms(cumulative, delta_head, tokens_head, scores, b_spans, c_spans, skip_gain):
    positions = jnp.arange(SPAN, dtype=jnp.int32)
    causal_mask = positions[:, None] >= positions[None, :]
    spread = cumulative[:, :, None] - cumulative[:, None, :]
    decays = jnp.exp(jnp.where(causal_mask[None], spread, -1e30))
    weights = (scores * decays * delta_head[:, None, :]).astype(jnp.bfloat16)
    weights = lax.optimization_barrier(weights).astype(jnp.float32)
    within = jnp.einsum("kts,ksp->ktp", weights, tokens_head)
    ending = cumulative[:, -1:]
    scaled_b = (b_spans * (jnp.exp(ending - cumulative) * delta_head)[:, :, None]).astype(jnp.bfloat16)
    scaled_b = lax.optimization_barrier(scaled_b).astype(jnp.float32)
    span_state = jnp.einsum("ksn,ksp->knp", scaled_b, tokens_head)
    span_decay = jnp.exp(ending[:, 0])

    def advance(state_now, pieces):
        factor, update = pieces
        return factor * state_now + update, state_now

    zero_state = jnp.zeros(span_state.shape[1:], jnp.float32)
    final_state, entering = lax.scan(advance, zero_state, (span_decay, span_state))
    entering_b = lax.optimization_barrier(entering.astype(jnp.bfloat16)).astype(jnp.float32)
    carried = jnp.einsum("ktn,knp->ktp", c_spans, entering_b) * jnp.exp(cumulative)[:, :, None]
    return (within + carried + skip_gain * tokens_head).astype(jnp.bfloat16)


def reference(inputs, b_panel, c_panel, dt_raw, dt_bias, a_log, d_skip):
    length = inputs.shape[0]
    blocks = length // SPAN
    delta = jax.nn.softplus(dt_raw.astype(jnp.float32) + dt_bias[None, :])
    rates = -jnp.exp(a_log)[None, :] * delta
    cumulative = jnp.cumsum(rates.reshape(blocks, SPAN, HEADS), axis=1)
    delta_blocks = delta.reshape(blocks, SPAN, HEADS)
    b_spans = b_panel.astype(jnp.float32).reshape(blocks, SPAN, DSTATE)
    c_spans = c_panel.astype(jnp.float32).reshape(blocks, SPAN, DSTATE)
    scores = jnp.einsum("ktn,ksn->kts", c_spans, b_spans)
    tokens_all = inputs.reshape(blocks, SPAN, HEADS, HDIM)

    def one_head(head):
        tokens_head = lax.dynamic_index_in_dim(tokens_all, head, 2, keepdims=False).astype(jnp.float32)
        cum_head = lax.dynamic_index_in_dim(cumulative, head, 2, keepdims=False)
        delta_head = lax.dynamic_index_in_dim(delta_blocks, head, 2, keepdims=False)
        skip_gain = lax.dynamic_index_in_dim(d_skip, head, 0, keepdims=False)
        return span_terms(cum_head, delta_head, tokens_head, scores, b_spans, c_spans, skip_gain)

    outputs = lax.map(one_head, jnp.arange(HEADS, dtype=jnp.int32))
    return jnp.transpose(outputs, (1, 2, 0, 3)).reshape(length, HEADS * HDIM)
```

```python
import functools

import jax
import jax.numpy as jnp
from jax import lax
from jax.experimental import pallas as pl
from jax.experimental.pallas import tpu as pltpu
from jax.sharding import PartitionSpec as P

HEADS = 128
HDIM = 64
DSTATE = 128
TOK = 320
PIECES = HEADS // 2
LOG2E = 1.4426950408889634
F32 = jnp.float32
BF16 = jnp.bfloat16
VMEM_LIMIT = 56 * 1024 * 1024


def state_kernel(x_ref, b_ref, c_ref, dt_ref, bias_ref, alog_ref, l_ref, a_ref, rt_ref, sm_ref, g_ref, bt_ref):
    step = pl.program_id(0)

    @pl.when(step == 0)
    def _():
        v = dt_ref[...].astype(F32) + bias_ref[...]
        delta = jnp.maximum(v, 0.0) + jnp.log(1.0 + jnp.exp(-jnp.abs(v)))
        rates = (-LOG2E) * jnp.exp(alog_ref[...]) * delta
        row = lax.broadcasted_iota(jnp.int32, (TOK, TOK), 0)
        col = lax.broadcasted_iota(jnp.int32, (TOK, TOK), 1)
        lower = (row >= col).astype(F32)
        a = jnp.dot(lower, rates, precision=lax.Precision.HIGHEST, preferred_element_type=F32)
        a_ref[...] = a
        r = a - jnp.log2(delta)
        rt_ref[...] = r.T
        g_ref[...] = (jnp.exp2(a[TOK - 1 : TOK, :] - a) * delta).astype(BF16)
        scores = lax.dot_general(c_ref[...], b_ref[...], (((1,), (1,)), ((), ())), preferred_element_type=F32)
        sm_ref[...] = jnp.where(row >= col, scores, 0.0)
        bt_ref[...] = b_ref[...].astype(F32).T.astype(BF16)

    width = x_ref.shape[1]
    row = lax.broadcasted_iota(jnp.int32, (HEADS, width), 0)
    col = lax.broadcasted_iota(jnp.int32, (HEADS, width), 1)
    spread = (row == step * (width // HDIM) + col // HDIM).astype(BF16)
    gain = jnp.dot(g_ref[...], spread, preferred_element_type=F32)
    scaled = (x_ref[...].astype(F32) * gain).astype(BF16)
    state = jnp.dot(bt_ref[...], scaled, preferred_element_type=F32).astype(BF16)
    for p in range(width // 128):
        l_ref[p] = state[:, 128 * p : 128 * (p + 1)]


def state_call(x, b, c, dt, bias, alog):
    steps = 8
    width = HEADS * HDIM // steps
    whole = lambda shape: pl.BlockSpec(shape, lambda i: (0,) * len(shape))
    return pl.pallas_call(
        state_kernel,
        grid=(steps,),
        in_specs=[
            pl.BlockSpec((TOK, width), lambda i: (0, i)),
            whole((TOK, DSTATE)),
            whole((TOK, DSTATE)),
            whole((TOK, HEADS)),
            whole((1, HEADS)),
            whole((1, HEADS)),
        ],
        out_specs=[
            pl.BlockSpec((width // 128, DSTATE, 128), lambda i: (i, 0, 0)),
            whole((TOK, HEADS)),
            whole((HEADS, TOK)),
            whole((TOK, TOK)),
        ],
        out_shape=[
            jax.ShapeDtypeStruct((PIECES, DSTATE, 128), BF16),
            jax.ShapeDtypeStruct((TOK, HEADS), F32),
            jax.ShapeDtypeStruct((HEADS, TOK), F32),
            jax.ShapeDtypeStruct((TOK, TOK), F32),
        ],
        scratch_shapes=[pltpu.VMEM((TOK, HEADS), BF16), pltpu.VMEM((DSTATE, TOK), BF16)],
        compiler_params=pltpu.CompilerParams(vmem_limit_bytes=VMEM_LIMIT),
        name="local_state",
    )(x, b, c, dt, bias, alog)


def scan_kernel(l_ref, d_ref, e_ref):
    def body(s, run):
        e_ref[s] = run.astype(BF16)
        return d_ref[pl.ds(s, 1), :] * run + l_ref[s].astype(F32)

    lax.fori_loop(0, l_ref.shape[0], body, jnp.zeros(l_ref.shape[1:], F32), unroll=4)


def out_kernel(x_ref, e_ref, c_ref, a_ref, rt_ref, sm_ref, skip_ref, o_ref):
    step = pl.program_id(0)
    pieces = x_ref.shape[1] // 128
    lane = lax.broadcasted_iota(jnp.int32, (TOK, 128), 1)
    first = lane < HDIM

    def body(p, carry):
        head = (step * pieces + p) * 2
        at = pl.ds(pl.multiple_of(p * 128, 128), 128)
        x = x_ref[:, at]
        turned = pltpu.roll(a_ref[...], lax.rem(HEADS - head, HEADS), 1)
        columns, parts = [], []
        for k in range(2):
            column = jnp.broadcast_to(turned[:, k : k + 1], (TOK, 128))
            columns.append(column)
            r = rt_ref[pl.ds(head + k, 1), :]
            rows = []
            for t0, t1 in ((0, 128), (128, 256), (256, TOK)):
                tiles = []
                for s0 in range(0, t1, 128):
                    s1 = min(s0 + 128, t1)
                    gap = column[t0:t1, : s1 - s0] - r[:, s0:s1]
                    if s1 > t0:
                        gap = jnp.minimum(gap, 100.0)
                    tiles.append((sm_ref[t0:t1, s0:s1] * jnp.exp2(gap)).astype(BF16))
                w = jnp.concatenate(tiles, axis=1) if len(tiles) > 1 else tiles[0]
                rows.append(jnp.dot(w, x[:t1], preferred_element_type=F32))
            parts.append(jnp.concatenate(rows, axis=0))
        within = jnp.where(first, parts[0], parts[1])
        fade = jnp.exp2(jnp.where(first, columns[0], columns[1]))
        carried = jnp.dot(c_ref[...], e_ref[p], preferred_element_type=F32)
        skip = jnp.where(first, skip_ref[0, head], skip_ref[0, head + 1])
        o_ref[:, at] = (within + carried * fade + skip * x.astype(F32)).astype(BF16)
        return carry

    lax.fori_loop(0, pieces, body, 0)


def out_call(x, e, c, a, rt, sm, skip):
    steps = 8
    width = HEADS * HDIM // steps
    whole = lambda shape: pl.BlockSpec(shape, lambda i: (0,) * len(shape))
    return pl.pallas_call(
        out_kernel,
        grid=(steps,),
        in_specs=[
            pl.BlockSpec((TOK, width), lambda i: (0, i)),
            pl.BlockSpec((width // 128, DSTATE, 128), lambda i: (i, 0, 0)),
            whole((TOK, DSTATE)),
            whole((TOK, HEADS)),
            whole((HEADS, TOK)),
            whole((TOK, TOK)),
            pl.BlockSpec(memory_space=pltpu.SMEM),
        ],
        out_specs=pl.BlockSpec((TOK, width), lambda i: (0, i)),
        out_shape=jax.ShapeDtypeStruct((TOK, HEADS * HDIM), BF16),
        compiler_params=pltpu.CompilerParams(vmem_limit_bytes=VMEM_LIMIT),
        name="outputs",
    )(x, e, c, a, rt, sm, skip)


def on_device(inputs, b_panel, c_panel, dt_raw, dt_bias, a_log, d_skip):
    axes = ("seq", "head")
    n = lax.axis_size(axes)
    states, a, rt, sm = state_call(inputs, b_panel, c_panel, dt_raw, dt_bias[None], a_log[None])
    share = PIECES * DSTATE // n
    ends = lax.all_gather(a[TOK - 1], axes, axis=0)
    mine = lax.all_to_all(states.reshape(n, share, 128), axes, 0, 0, tiled=True)
    here = lax.axis_index("seq") * lax.axis_size("head") + lax.axis_index("head")
    piece = here * share // DSTATE
    decay = jnp.repeat(jnp.exp2(lax.dynamic_slice_in_dim(ends, 2 * piece, 2, 1)), HDIM, axis=1)
    entering = pl.pallas_call(
        scan_kernel,
        out_shape=jax.ShapeDtypeStruct(mine.shape, BF16),
        compiler_params=pltpu.CompilerParams(vmem_limit_bytes=VMEM_LIMIT),
        name="scan_devices",
    )(mine, decay)
    entering = lax.all_to_all(entering, axes, 0, 0, tiled=True).reshape(PIECES, DSTATE, 128)
    return out_call(inputs, entering, c_panel, a, rt, sm, d_skip[None])


def solution(mesh):
    return jax.shard_map(
        on_device,
        mesh=mesh,
        in_specs=(P(("seq", "head"), None),) * 4 + (P(), P(), P()),
        out_specs=P(("seq", "head"), None),
        check_vma=False,
    )
```

```python
import functools

import jax
import jax.numpy as jnp
from jax import lax
from jax.experimental import pallas as pl
from jax.experimental.pallas import tpu as pltpu
from jax.sharding import PartitionSpec as P

HEADS = 128
HDIM = 64
DSTATE = 128
TOK = 320
PIECES = HEADS // 2
LOG2E = 1.4426950408889634
F32 = jnp.float32
BF16 = jnp.bfloat16
VMEM_LIMIT = 56 * 1024 * 1024


def state_kernel(x_ref, b_ref, c_ref, dt_ref, bias_ref, alog_ref, l_ref, a_ref, rt_ref, sm_ref, g_ref, bt_ref):
    step = pl.program_id(0)

    @pl.when(step == 0)
    def _():
        v = dt_ref[...].astype(F32) + bias_ref[...]
        delta = jnp.maximum(v, 0.0) + jnp.log(1.0 + jnp.exp(-jnp.abs(v)))
        rates = (-LOG2E) * jnp.exp(alog_ref[...]) * delta
        row = lax.broadcasted_iota(jnp.int32, (TOK, TOK), 0)
        col = lax.broadcasted_iota(jnp.int32, (TOK, TOK), 1)
        lower = (row >= col).astype(F32)
        a = jnp.dot(lower, rates, precision=lax.Precision.HIGHEST, preferred_element_type=F32)
        a_ref[...] = a
        r = a - jnp.log2(delta)
        rt_ref[...] = r.T
        g_ref[...] = (jnp.exp2(a[TOK - 1 : TOK, :] - a) * delta).astype(BF16)
        scores = lax.dot_general(c_ref[...], b_ref[...], (((1,), (1,)), ((), ())), preferred_element_type=F32)
        sm_ref[...] = jnp.where(row >= col, scores, 0.0)
        bt_ref[...] = b_ref[...].astype(F32).T.astype(BF16)

    width = x_ref.shape[1]
    row = lax.broadcasted_iota(jnp.int32, (HEADS, width), 0)
    col = lax.broadcasted_iota(jnp.int32, (HEADS, width), 1)
    spread = (row == step * (width // HDIM) + col // HDIM).astype(BF16)
    gain = jnp.dot(g_ref[...], spread, preferred_element_type=F32)
    scaled = (x_ref[...].astype(F32) * gain).astype(BF16)
    state = jnp.dot(bt_ref[...], scaled, preferred_element_type=F32).astype(BF16)
    for p in range(width // 128):
        l_ref[p] = state[:, 128 * p : 128 * (p + 1)]


def state_call(x, b, c, dt, bias, alog):
    steps = 8
    width = HEADS * HDIM // steps
    whole = lambda shape: pl.BlockSpec(shape, lambda i: (0,) * len(shape))
    return pl.pallas_call(
        state_kernel,
        grid=(steps,),
        in_specs=[
            pl.BlockSpec((TOK, width), lambda i: (0, i)),
            whole((TOK, DSTATE)),
            whole((TOK, DSTATE)),
            whole((TOK, HEADS)),
            whole((1, HEADS)),
            whole((1, HEADS)),
        ],
        out_specs=[
            pl.BlockSpec((width // 128, DSTATE, 128), lambda i: (i, 0, 0)),
            whole((TOK, HEADS)),
            whole((HEADS, TOK)),
            whole((TOK, TOK)),
        ],
        out_shape=[
            jax.ShapeDtypeStruct((PIECES, DSTATE, 128), BF16),
            jax.ShapeDtypeStruct((TOK, HEADS), F32),
            jax.ShapeDtypeStruct((HEADS, TOK), F32),
            jax.ShapeDtypeStruct((TOK, TOK), F32),
        ],
        scratch_shapes=[pltpu.VMEM((TOK, HEADS), BF16), pltpu.VMEM((DSTATE, TOK), BF16)],
        compiler_params=pltpu.CompilerParams(vmem_limit_bytes=VMEM_LIMIT),
        name="local_state",
    )(x, b, c, dt, bias, alog)


def link_kernel(cfg, l_ref, a_ref, fl, fr, fe, sl, sr, rs, rbuf, eb, za, pa, dec_own, dec_pre, dec_suf, rowdec,
                fl_sem, fr_sem, fe_sem, left_sem, right_sem, rs_sem, rbuf_sem, eb_sem, z_send, z_recv, p_send, p_recv):
    Z, Y, R, K, A, B, C = cfg
    low = Z // 2 - 1
    seq = lax.axis_index("seq")
    head = lax.axis_index("head")
    y = head // Z
    z = head - y * Z
    r = seq * Y + y
    in_plane = (z == low) | (z == low + 1)
    scan_piece = 2 * r + (z - low)

    def remote(src, dst, send, recv, to_seq, to_head):
        return pltpu.make_async_remote_copy(
            src_ref=src, dst_ref=dst, send_sem=send, recv_sem=recv,
            device_id={"seq": to_seq, "head": to_head}, device_id_type=pl.DeviceIdType.MESH,
        )

    def await_bytes(ref, sem):
        pltpu.make_async_copy(ref, ref, sem).wait()

    def send_left(src, q):
        remote(src, fr.at[q], left_sem, fr_sem.at[q], seq, head - 1).start()

    def send_right(src, q):
        remote(src, fl.at[q], right_sem, fl_sem.at[q], seq, head + 1).start()

    za[pl.ds(pl.multiple_of(z * 8, 8), 8), :] = jnp.broadcast_to(a_ref[TOK - 1 : TOK, :], (8, 128))
    mine = za.at[pl.ds(pl.multiple_of(z * 8, 8), 8), :]
    for dz in range(1, Z):
        remote(mine, mine, z_send, z_recv, seq, y * Z + lax.rem(z + dz, Z)).start()
    await_bytes(za.at[0 : 8 * (Z - 1), :], z_recv)
    own = za[pl.ds(pl.multiple_of(z * 8, 8), 8), :]
    before = jnp.zeros((8, 128), F32)
    after = jnp.zeros((8, 128), F32)
    for other in range(Z):
        value = za[8 * other : 8 * other + 8, :]
        before = before + jnp.where(other < z, value, 0.0)
        after = after + jnp.where(other > z, value, 0.0)

    @pl.when(in_plane)
    def _():
        slot = pl.ds(pl.multiple_of(r * 8, 8), 8)
        pa[slot, :] = before + own + after

        def tell(d, carry):
            to = lax.rem(r + d, R)
            to_seq = to // Y
            remote(pa.at[slot, :], pa.at[slot, :], p_send, p_recv, to_seq, (to - to_seq * Y) * Z + z).start()
            return carry

        lax.fori_loop(1, R, tell, 0)

    piece_at = lax.broadcasted_iota(jnp.int32, (K, 128), 0)
    head_at = lax.broadcasted_iota(jnp.int32, (K, 128), 1)
    pick_head = lax.broadcasted_iota(jnp.int32, (128, 128), 0)
    pick_lane = lax.broadcasted_iota(jnp.int32, (128, 128), 1) // HDIM
    second = (lax.rem(pick_head, 2) == pick_lane).astype(F32)
    for value, out in ((own, dec_own), (before, dec_pre), (after, dec_suf)):
        only = jnp.where(head_at // 2 == piece_at, value[0:1, :], 0.0)
        logs = jnp.dot(only, second, precision=lax.Precision.HIGHEST, preferred_element_type=F32)
        out[...] = jnp.exp2(logs)

    def tick(i, carry):
        for par in range(2):
            m = low + par
            q = i - (4 * A + B + C) - A * jnp.abs(z - m)
            at = jnp.clip(q, 0, K - 1)
            k = at // 2
            valid = (q >= 0) & (q < K) & (lax.rem(at, 2) == par)

            @pl.when(valid & (z < m))
            def _():
                remote(sl.at[at], fr.at[at], left_sem, fr_sem.at[at], seq, head + 1).wait_recv()

                @pl.when(z > 0)
                def _():
                    send_left(fr.at[at], at)
                    fl[at] = (fl[at].astype(F32) + dec_pre[pl.ds(at, 1), :] * fr[at].astype(F32)).astype(BF16)

                @pl.when(z == 0)
                def _():
                    fl[at] = fr[at]

            @pl.when(valid & (z == m))
            def _():
                @pl.when(k != r)
                def _():
                    to = lax.rem(r + 1, R)
                    to_seq = to // Y
                    remote(fe.at[k], fe.at[k], eb_sem, fe_sem.at[k], to_seq, (to - to_seq * Y) * Z + z).wait_recv()

                send_left(fe.at[k], at)
                entering = fl[at].astype(F32) + dec_pre[pl.ds(at, 1), :] * fe[k].astype(F32)
                fl[at] = entering.astype(BF16)
                sr[at] = (dec_own[pl.ds(at, 1), :] * entering + l_ref[at].astype(F32)).astype(BF16)
                send_right(sr.at[at], at)

            @pl.when(valid & (z > m))
            def _():
                remote(sr.at[at], fl.at[at], right_sem, fl_sem.at[at], seq, head - 1).wait_recv()

                @pl.when(z < Z - 1)
                def _():
                    sr[at] = (dec_own[pl.ds(at, 1), :] * fl[at].astype(F32) + l_ref[at].astype(F32)).astype(BF16)
                    send_right(sr.at[at], at)

        q = i - A * z
        at = jnp.clip(q, 0, K - 1)
        valid = (q >= 0) & (q < K) & (z < low + lax.rem(at, 2))

        @pl.when(valid & (z == 0))
        def _():
            send_right(l_ref.at[at], at)

        @pl.when(valid & (z > 0))
        def _():
            remote(sr.at[at], fl.at[at], right_sem, fl_sem.at[at], seq, head - 1).wait_recv()
            sr[at] = (dec_own[pl.ds(at, 1), :] * fl[at].astype(F32) + l_ref[at].astype(F32)).astype(BF16)
            send_right(sr.at[at], at)

        q1 = i - A * (Z - 1 - z)
        at1 = jnp.clip(q1, 0, K - 1)
        valid1 = (q1 >= 0) & (q1 < K) & (z > low + lax.rem(at1, 2))

        @pl.when(valid1 & (z == Z - 1))
        def _():
            send_left(l_ref.at[at1], at1)

        @pl.when(valid1 & (z < Z - 1))
        def _():
            remote(sl.at[at1], fr.at[at1], left_sem, fr_sem.at[at1], seq, head + 1).wait_recv()
            sl[at1] = (dec_suf[pl.ds(at1, 1), :] * l_ref[at1].astype(F32) + fr[at1].astype(F32)).astype(BF16)
            send_left(sl.at[at1], at1)

        q2 = i - 4 * A
        at2 = jnp.clip(q2, 0, K - 1)
        k2 = at2 // 2

        @pl.when((q2 >= 0) & (q2 < K) & (z == low + lax.rem(at2, 2)))
        def _():
            remote(sr.at[at2], fl.at[at2], right_sem, fl_sem.at[at2], seq, head - 1).wait_recv()
            remote(sl.at[at2], fr.at[at2], left_sem, fr_sem.at[at2], seq, head + 1).wait_recv()
            inner = dec_own[pl.ds(at2, 1), :] * fl[at2].astype(F32) + l_ref[at2].astype(F32)
            total = (dec_suf[pl.ds(at2, 1), :] * inner + fr[at2].astype(F32)).astype(BF16)

            @pl.when(k2 == r)
            def _():
                rbuf[r] = total

            @pl.when(k2 != r)
            def _():
                rs[k2] = total
                to_seq = k2 // Y
                remote(rs.at[k2], rbuf.at[r], rs_sem, rbuf_sem, to_seq, (k2 - to_seq * Y) * Z + z).start()

        @pl.when(in_plane & (i == scan_piece + 4 * A + B))
        def _():
            await_bytes(pa.at[0 : 8 * (R - 1), :], p_recv)
            chosen = (pick_head == 2 * scan_piece + pick_lane).astype(F32)
            rowdec[...] = jnp.exp2(
                jnp.dot(pa[...], chosen, precision=lax.Precision.HIGHEST, preferred_element_type=F32)
            )
            await_bytes(rbuf.at[0 : R - 1], rbuf_sem)

            def row(s, run):
                e = run.astype(BF16)

                @pl.when(s == r)
                def _():
                    fe[r] = e

                @pl.when(s != r)
                def _():
                    eb[s] = e
                    to_seq = s // Y
                    remote(eb.at[s], fe.at[r], eb_sem, fe_sem.at[r], to_seq, (s - to_seq * Y) * Z + z).start()

                return rowdec[pl.ds(s * 8, 1), :] * run + rbuf[s].astype(F32)

            lax.fori_loop(0, R, row, jnp.zeros((DSTATE, 128), F32))

        return carry

    lax.fori_loop(0, K + 4 * A + B + C + A * (Z // 2), tick, 0)

    await_bytes(za.at[0 : 8 * (Z - 1), :], z_send)

    @pl.when(z > 0)
    def _():
        await_bytes(sl, left_sem)

    @pl.when(z < Z - 1)
    def _():
        await_bytes(sr, right_sem)

    @pl.when(in_plane)
    def _():
        await_bytes(pa.at[0 : 8 * (R - 1), :], p_send)
        await_bytes(rbuf.at[0 : R - 1], rs_sem)
        await_bytes(rbuf.at[0 : R - 1], eb_sem)


def link_call(states, a, Z=8, K=PIECES, A=3, B=6, C=6):
    Y = lax.axis_size("head") // Z
    R = lax.axis_size("seq") * Y
    tile = (DSTATE, 128)
    dma = pltpu.SemaphoreType.DMA
    return pl.pallas_call(
        functools.partial(link_kernel, (Z, Y, R, K, A, B, C)),
        in_specs=[pl.BlockSpec(memory_space=pltpu.VMEM)] * 2,
        out_specs=pl.BlockSpec(memory_space=pltpu.VMEM),
        out_shape=jax.ShapeDtypeStruct((K, *tile), BF16),
        scratch_shapes=[
            pltpu.VMEM((K, *tile), BF16),
            pltpu.VMEM((K // 2, *tile), BF16),
            pltpu.VMEM((K, *tile), BF16),
            pltpu.VMEM((K, *tile), BF16),
            pltpu.VMEM((K // 2, *tile), BF16),
            pltpu.VMEM((R, *tile), BF16),
            pltpu.VMEM((R, *tile), BF16),
            pltpu.VMEM((Z * 8, 128), F32),
            pltpu.VMEM((R * 8, 128), F32),
            pltpu.VMEM((K, 128), F32),
            pltpu.VMEM((K, 128), F32),
            pltpu.VMEM((K, 128), F32),
            pltpu.VMEM((R * 8, 128), F32),
            dma((K,)), dma((K,)), dma((K // 2,)),
            dma, dma, dma, dma, dma, dma, dma, dma, dma,
        ],
        compiler_params=pltpu.CompilerParams(vmem_limit_bytes=VMEM_LIMIT, has_side_effects=True),
        name="link_states",
    )(states, a)


def out_kernel(x_ref, e_ref, c_ref, a_ref, rt_ref, sm_ref, skip_ref, o_ref):
    step = pl.program_id(0)
    pieces = x_ref.shape[1] // 128
    lane = lax.broadcasted_iota(jnp.int32, (TOK, 128), 1)
    first = lane < HDIM

    def body(p, carry):
        head = (step * pieces + p) * 2
        at = pl.ds(pl.multiple_of(p * 128, 128), 128)
        x = x_ref[:, at]
        turned = pltpu.roll(a_ref[...], lax.rem(HEADS - head, HEADS), 1)
        columns, parts = [], []
        for k in range(2):
            column = jnp.broadcast_to(turned[:, k : k + 1], (TOK, 128))
            columns.append(column)
            r = rt_ref[pl.ds(head + k, 1), :]
            rows = []
            for t0, t1 in ((0, 128), (128, 256), (256, TOK)):
                tiles = []
                for s0 in range(0, t1, 128):
                    s1 = min(s0 + 128, t1)
                    gap = column[t0:t1, : s1 - s0] - r[:, s0:s1]
                    if s1 > t0:
                        gap = jnp.minimum(gap, 100.0)
                    tiles.append((sm_ref[t0:t1, s0:s1] * jnp.exp2(gap)).astype(BF16))
                w = jnp.concatenate(tiles, axis=1) if len(tiles) > 1 else tiles[0]
                rows.append(jnp.dot(w, x[:t1], preferred_element_type=F32))
            parts.append(jnp.concatenate(rows, axis=0))
        within = jnp.where(first, parts[0], parts[1])
        fade = jnp.exp2(jnp.where(first, columns[0], columns[1]))
        carried = jnp.dot(c_ref[...], e_ref[p], preferred_element_type=F32)
        skip = jnp.where(first, skip_ref[0, head], skip_ref[0, head + 1])
        o_ref[:, at] = (within + carried * fade + skip * x.astype(F32)).astype(BF16)
        return carry

    lax.fori_loop(0, pieces, body, 0)


def out_call(x, e, c, a, rt, sm, skip):
    steps = 8
    width = HEADS * HDIM // steps
    whole = lambda shape: pl.BlockSpec(shape, lambda i: (0,) * len(shape))
    return pl.pallas_call(
        out_kernel,
        grid=(steps,),
        in_specs=[
            pl.BlockSpec((TOK, width), lambda i: (0, i)),
            pl.BlockSpec((width // 128, DSTATE, 128), lambda i: (i, 0, 0)),
            whole((TOK, DSTATE)),
            whole((TOK, HEADS)),
            whole((HEADS, TOK)),
            whole((TOK, TOK)),
            pl.BlockSpec(memory_space=pltpu.SMEM),
        ],
        out_specs=pl.BlockSpec((TOK, width), lambda i: (0, i)),
        out_shape=jax.ShapeDtypeStruct((TOK, HEADS * HDIM), BF16),
        compiler_params=pltpu.CompilerParams(vmem_limit_bytes=VMEM_LIMIT),
        name="outputs",
    )(x, e, c, a, rt, sm, skip)


def on_device(inputs, b_panel, c_panel, dt_raw, dt_bias, a_log, d_skip):
    states, a, rt, sm = state_call(inputs, b_panel, c_panel, dt_raw, dt_bias[None], a_log[None])
    entering = link_call(states, a)
    return out_call(inputs, entering, c_panel, a, rt, sm, d_skip[None])


def solution(mesh):
    return jax.shard_map(
        on_device,
        mesh=mesh,
        in_specs=(P(("seq", "head"), None),) * 4 + (P(), P(), P()),
        out_specs=P(("seq", "head"), None),
        check_vma=False,
    )
```

```python
import functools

import jax
import jax.numpy as jnp
from jax import lax
from jax.experimental import pallas as pl
from jax.experimental.pallas import tpu as pltpu
from jax.sharding import PartitionSpec as P

HEADS = 128
HDIM = 64
DSTATE = 128
TOK = 320
PIECES = HEADS // 2
PARTS = 4
TURNS = 4
XBLOCKS = 8
LOG2E = 1.4426950408889634
F32 = jnp.float32
BF16 = jnp.bfloat16
VMEM_LIMIT = 56 * 1024 * 1024


def layer_kernel(cfg, x_hbm, b_ref, c_ref, dt_ref, bias_ref, alog_ref, skip_ref, o_hbm,
                 x_ref, o_ref, part_ref, fade_ref, a_ref, rt_ref, sm_ref, g_ref, bt_ref,
                 l_ref, fl, fr, fe, sl, sr, rs, rbuf, eb, za, pa, dec_own, dec_pre, dec_suf, rowdec,
                 x_sem, o_sem, fl_sem, fr_sem, fe_sem, left_sem, right_sem, rs_sem, rbuf_sem, eb_sem,
                 z_send, z_recv, p_send, p_recv):
    Z, Y, R, K, A, B, C = cfg
    low = Z // 2 - 1
    seq = lax.axis_index("seq")
    head = lax.axis_index("head")
    y = head // Z
    z = head - y * Z
    r = seq * Y + y
    in_plane = (z == low) | (z == low + 1)
    part = lax.rem(r, PARTS)
    rows = DSTATE // PARTS

    def remote(src, dst, send, recv, to_seq, to_head):
        return pltpu.make_async_remote_copy(
            src_ref=src, dst_ref=dst, send_sem=send, recv_sem=recv,
            device_id={"seq": to_seq, "head": to_head}, device_id_type=pl.DeviceIdType.MESH,
        )

    def await_bytes(ref, sem):
        pltpu.make_async_copy(ref, ref, sem).wait()

    def send_left(src, q):
        remote(src, fr.at[q], left_sem, fr_sem.at[q], seq, head - 1).start()

    def send_right(src, q):
        remote(src, fl.at[q], right_sem, fl_sem.at[q], seq, head + 1).start()

    gate = pltpu.get_barrier_semaphore()

    def greet(to_seq, to_head):
        pl.semaphore_signal(
            gate, inc=1, device_id={"seq": to_seq, "head": to_head}, device_id_type=pl.DeviceIdType.MESH
        )

    for dz in range(1, Z):
        greet(seq, y * Z + lax.rem(z + dz, Z))

    @pl.when(in_plane)
    def _():
        def hello(d, carry):
            to = lax.rem(r + d, R)
            to_seq = to // Y
            greet(to_seq, (to - to_seq * Y) * Z + z)
            return carry

        lax.fori_loop(1, R, hello, 0)

    blocks = XBLOCKS
    width = K * 128 // blocks

    def x_copy(n):
        cols = pl.ds(pl.multiple_of(n * width, width), width)
        return pltpu.make_async_copy(x_hbm.at[:, cols], x_ref.at[:, cols], x_sem.at[n])

    for n in range(blocks):
        x_copy(n).start()

    v = dt_ref[...].astype(F32) + bias_ref[...]
    delta = jnp.maximum(v, 0.0) + jnp.log(1.0 + jnp.exp(-jnp.abs(v)))
    rates = (-LOG2E) * jnp.exp(alog_ref[...]) * delta
    t_at = lax.broadcasted_iota(jnp.int32, (TOK, TOK), 0)
    s_at = lax.broadcasted_iota(jnp.int32, (TOK, TOK), 1)
    lower = (t_at >= s_at).astype(F32)
    a = jnp.dot(lower, rates, precision=lax.Precision.HIGHEST, preferred_element_type=F32)
    a_ref[...] = a
    rt_ref[...] = (a - jnp.log2(delta)).T
    g_ref[...] = (jnp.exp2(a[TOK - 1 : TOK, :] - a) * delta).astype(BF16)
    scores = lax.dot_general(c_ref[...], b_ref[...], (((1,), (1,)), ((), ())), preferred_element_type=F32)
    sm_ref[...] = jnp.where(t_at >= s_at, scores, 0.0)
    bt_ref[...] = b_ref[...].astype(F32).T.astype(BF16)

    pl.semaphore_wait(gate, Z - 1 + jnp.where(in_plane, R - 1, 0))

    za[pl.ds(pl.multiple_of(z * 8, 8), 8), :] = jnp.broadcast_to(a_ref[TOK - 1 : TOK, :], (8, 128))
    mine = za.at[pl.ds(pl.multiple_of(z * 8, 8), 8), :]
    for dz in range(1, Z):
        remote(mine, mine, z_send, z_recv, seq, y * Z + lax.rem(z + dz, Z)).start()
    await_bytes(za.at[0 : 8 * (Z - 1), :], z_recv)
    own = za[pl.ds(pl.multiple_of(z * 8, 8), 8), :]
    before = jnp.zeros((8, 128), F32)
    after = jnp.zeros((8, 128), F32)
    for other in range(Z):
        value = za[8 * other : 8 * other + 8, :]
        before = before + jnp.where(other < z, value, 0.0)
        after = after + jnp.where(other > z, value, 0.0)

    @pl.when(in_plane)
    def _():
        slot = pl.ds(pl.multiple_of(r * 8, 8), 8)
        pa[slot, :] = before + own + after

        def tell(d, carry):
            to = lax.rem(r + d, R)
            to_seq = to // Y
            remote(pa.at[slot, :], pa.at[slot, :], p_send, p_recv, to_seq, (to - to_seq * Y) * Z + z).start()
            return carry

        lax.fori_loop(1, R, tell, 0)

    piece_at = lax.broadcasted_iota(jnp.int32, (K, 128), 0)
    head_at = lax.broadcasted_iota(jnp.int32, (K, 128), 1)
    pick_head = lax.broadcasted_iota(jnp.int32, (128, 128), 0)
    pick_lane = lax.broadcasted_iota(jnp.int32, (128, 128), 1) // HDIM
    second = (lax.rem(pick_head, 2) == pick_lane).astype(F32)
    for value, out in ((own, dec_own), (before, dec_pre), (after, dec_suf)):
        only = jnp.where(head_at // 2 == piece_at, value[0:1, :], 0.0)
        logs = jnp.dot(only, second, precision=lax.Precision.HIGHEST, preferred_element_type=F32)
        out[...] = jnp.exp2(logs)

    lane = lax.broadcasted_iota(jnp.int32, (TOK, 128), 1)
    first = lane < HDIM

    def columns_of(q):
        return pl.ds(pl.multiple_of(q * 128, 128), 128)

    def local_state(q):
        spread = (pick_head == 2 * q + pick_lane).astype(BF16)
        gain = jnp.dot(g_ref[...], spread, preferred_element_type=F32)
        scaled = (x_ref[:, columns_of(q)].astype(F32) * gain).astype(BF16)
        l_ref[q] = jnp.dot(bt_ref[...], scaled, preferred_element_type=F32).astype(BF16)

    def within_and_skip(q):
        x = x_ref[:, columns_of(q)]
        turned = pltpu.roll(a_ref[...], lax.rem(HEADS - 2 * q, HEADS), 1)
        columns, parts = [], []
        for k in range(2):
            column = jnp.broadcast_to(turned[:, k : k + 1], (TOK, 128))
            columns.append(column)
            row = rt_ref[pl.ds(2 * q + k, 1), :]
            outs = []
            for t0, t1 in ((0, 128), (128, 256), (256, TOK)):
                tiles = []
                for s0 in range(0, t1, 128):
                    s1 = min(s0 + 128, t1)
                    gap = column[t0:t1, : s1 - s0] - row[:, s0:s1]
                    if s1 > t0:
                        gap = jnp.minimum(gap, 100.0)
                    tiles.append((sm_ref[t0:t1, s0:s1] * jnp.exp2(gap)).astype(BF16))
                w = jnp.concatenate(tiles, axis=1) if len(tiles) > 1 else tiles[0]
                outs.append(jnp.dot(w, x[:t1], preferred_element_type=F32))
            parts.append(jnp.concatenate(outs, axis=0))
        fade_ref[q] = jnp.exp2(jnp.where(first, columns[0], columns[1]))
        skip = jnp.where(first, skip_ref[0, 2 * q], skip_ref[0, 2 * q + 1])
        part_ref[q] = jnp.where(first, parts[0], parts[1]) + skip * x.astype(F32)

    def finish(q):
        carried = jnp.dot(c_ref[...], fl[q], preferred_element_type=F32)
        o_ref[:, columns_of(q)] = (part_ref[q] + fade_ref[q] * carried).astype(BF16)
        pltpu.make_async_copy(o_ref.at[:, columns_of(q)], o_hbm.at[:, columns_of(q)], o_sem).start()

    def tick(i, carry):
        for par in range(2):
            m = low + par
            q = i - (4 * A + B + C) - A * jnp.abs(z - m)
            at = jnp.clip(q, 0, K - 1)
            k = at // 2
            valid = (q >= 0) & (q < K) & (lax.rem(at, 2) == par)

            @pl.when(valid & (z < m))
            def _():
                remote(sl.at[at], fr.at[at], left_sem, fr_sem.at[at], seq, head + 1).wait_recv()

                @pl.when(z > 0)
                def _():
                    send_left(fr.at[at], at)
                    fl[at] = (fl[at].astype(F32) + dec_pre[pl.ds(at, 1), :] * fr[at].astype(F32)).astype(BF16)

                @pl.when(z == 0)
                def _():
                    fl[at] = fr[at]

            @pl.when(valid & (z == m))
            def _():
                mine = r // PARTS == lax.rem(k, R // PARTS)

                @pl.when(mine)
                def _():
                    await_bytes(fe.at[k, 0 : rows * (PARTS - 1)], fe_sem.at[k])

                @pl.when(jnp.logical_not(mine))
                def _():
                    await_bytes(fe.at[k], fe_sem.at[k])

                send_left(fe.at[k], at)
                entering = fl[at].astype(F32) + dec_pre[pl.ds(at, 1), :] * fe[k].astype(F32)
                fl[at] = entering.astype(BF16)
                sr[at] = (dec_own[pl.ds(at, 1), :] * entering + l_ref[at].astype(F32)).astype(BF16)
                send_right(sr.at[at], at)

            @pl.when(valid & (z > m))
            def _():
                remote(sr.at[at], fl.at[at], right_sem, fl_sem.at[at], seq, head - 1).wait_recv()

                @pl.when(z < Z - 1)
                def _():
                    sr[at] = (dec_own[pl.ds(at, 1), :] * fl[at].astype(F32) + l_ref[at].astype(F32)).astype(BF16)
                    send_right(sr.at[at], at)

        ahead = jnp.minimum(i, K - 1)
        per_block = K // XBLOCKS

        @pl.when((i < K) & (lax.rem(ahead, per_block) == 0))
        def _():
            x_copy(ahead // per_block).wait()

        @pl.when(i < K)
        def _():
            local_state(ahead)

        q = i - A * z
        at = jnp.clip(q, 0, K - 1)
        valid = (q >= 0) & (q < K) & (z < low + lax.rem(at, 2))

        @pl.when(valid & (z == 0))
        def _():
            send_right(l_ref.at[at], at)

        @pl.when(valid & (z > 0))
        def _():
            remote(sr.at[at], fl.at[at], right_sem, fl_sem.at[at], seq, head - 1).wait_recv()
            sr[at] = (dec_own[pl.ds(at, 1), :] * fl[at].astype(F32) + l_ref[at].astype(F32)).astype(BF16)
            send_right(sr.at[at], at)

        q1 = i - A * (Z - 1 - z)
        at1 = jnp.clip(q1, 0, K - 1)
        valid1 = (q1 >= 0) & (q1 < K) & (z > low + lax.rem(at1, 2))

        @pl.when(valid1 & (z == Z - 1))
        def _():
            send_left(l_ref.at[at1], at1)

        @pl.when(valid1 & (z < Z - 1))
        def _():
            remote(sl.at[at1], fr.at[at1], left_sem, fr_sem.at[at1], seq, head + 1).wait_recv()
            sl[at1] = (dec_suf[pl.ds(at1, 1), :] * l_ref[at1].astype(F32) + fr[at1].astype(F32)).astype(BF16)
            send_left(sl.at[at1], at1)

        q2 = i - 4 * A
        at2 = jnp.clip(q2, 0, K - 1)
        k2 = at2 // 2

        @pl.when((q2 >= 0) & (q2 < K) & (z == low + lax.rem(at2, 2)))
        def _():
            remote(sr.at[at2], fl.at[at2], right_sem, fl_sem.at[at2], seq, head - 1).wait_recv()
            remote(sl.at[at2], fr.at[at2], left_sem, fr_sem.at[at2], seq, head + 1).wait_recv()
            inner = dec_own[pl.ds(at2, 1), :] * fl[at2].astype(F32) + l_ref[at2].astype(F32)
            total = (dec_suf[pl.ds(at2, 1), :] * inner + fr[at2].astype(F32)).astype(BF16)

            rs[k2] = total
            base = lax.rem(k2, R // PARTS) * PARTS
            turn = k2 // (R // PARTS)
            for p in range(PARTS):
                to = base + p

                @pl.when(to == r)
                def _():
                    rbuf[turn, r] = total[rows * p : rows * (p + 1)]

                @pl.when(to != r)
                def _():
                    to_seq = to // Y
                    remote(
                        rs.at[k2, rows * p : rows * (p + 1)], rbuf.at[turn, r], rs_sem, rbuf_sem.at[turn],
                        to_seq, (to - to_seq * Y) * Z + z,
                    ).start()

        @pl.when(in_plane & (i == 4 * A))
        def _():
            await_bytes(pa.at[0 : 8 * (R - 1), :], p_recv)

        for turn in range(TURNS):
            k3 = r // PARTS + turn * (R // PARTS)
            q3 = 2 * k3 + (z - low)

            @pl.when(in_plane & (i == q3 + 4 * A + B))
            def _():
                chosen = (pick_head == 2 * q3 + pick_lane).astype(F32)
                rowdec[...] = jnp.exp2(
                    jnp.dot(pa[...], chosen, precision=lax.Precision.HIGHEST, preferred_element_type=F32)
                )
                await_bytes(rbuf.at[turn, 0 : R - 1], rbuf_sem.at[turn])
                span = pl.ds(pl.multiple_of(part * rows, rows), rows)

                def row(s, run):
                    e = run.astype(BF16)

                    @pl.when(s == r)
                    def _():
                        fe[k3, span] = e

                    @pl.when(s != r)
                    def _():
                        eb[turn, s] = e
                        to_seq = s // Y
                        remote(
                            eb.at[turn, s], fe.at[k3, span], eb_sem, fe_sem.at[k3],
                            to_seq, (s - to_seq * Y) * Z + z,
                        ).start()

                    return rowdec[pl.ds(s * 8, 1), :] * run + rbuf[turn, s].astype(F32)

                lax.fori_loop(0, R, row, jnp.zeros((rows, 128), F32))

        w = i // 3 * 2 + lax.rem(i, 3)
        w_at = jnp.minimum(w, K - 1)

        @pl.when((lax.rem(i, 3) < 2) & (w < K))
        def _():
            within_and_skip(w_at)

        for par in range(2):
            q = i - (4 * A + B + C) - A * jnp.abs(z - low - par)
            at = jnp.clip(q, 0, K - 1)

            @pl.when((q >= 0) & (q < K) & (lax.rem(at, 2) == par))
            def _():
                finish(at)

        return carry

    lax.fori_loop(0, K + 4 * A + B + C + A * (Z // 2), tick, 0)

    pltpu.make_async_copy(o_ref, o_hbm, o_sem).wait()
    await_bytes(za.at[0 : 8 * (Z - 1), :], z_send)

    @pl.when(z > 0)
    def _():
        await_bytes(sl, left_sem)

    @pl.when(z < Z - 1)
    def _():
        await_bytes(sr, right_sem)

    @pl.when(in_plane)
    def _():
        await_bytes(pa.at[0 : 8 * (R - 1), :], p_send)
        for turn in range(TURNS):
            await_bytes(rbuf.at[turn, 0 : R - 1], rs_sem)
            await_bytes(rbuf.at[turn, 0 : R - 1], eb_sem)


def layer_call(x, b, c, dt, bias, alog, skip, Z=8, K=PIECES, A=6, B=8, C=10):
    Y = lax.axis_size("head") // Z
    R = lax.axis_size("seq") * Y
    tile = (DSTATE, 128)
    dma = pltpu.SemaphoreType.DMA
    vmem = pl.BlockSpec(memory_space=pltpu.VMEM)
    hbm = pl.BlockSpec(memory_space=pl.ANY)
    small = pltpu.VMEM((R * 8, 128), F32)
    share = pltpu.VMEM((TURNS, R, DSTATE // PARTS, 128), BF16)
    return pl.pallas_call(
        functools.partial(layer_kernel, (Z, Y, R, K, A, B, C)),
        in_specs=[hbm, vmem, vmem, vmem, vmem, vmem, pl.BlockSpec(memory_space=pltpu.SMEM)],
        out_specs=hbm,
        out_shape=jax.ShapeDtypeStruct((TOK, K * 128), BF16),
        scratch_shapes=[
            pltpu.VMEM((TOK, K * 128), BF16),
            pltpu.VMEM((TOK, K * 128), BF16),
            pltpu.VMEM((K, TOK, 128), F32),
            pltpu.VMEM((K, TOK, 128), F32),
            pltpu.VMEM((TOK, HEADS), F32),
            pltpu.VMEM((HEADS, TOK), F32),
            pltpu.VMEM((TOK, TOK), F32),
            pltpu.VMEM((TOK, HEADS), BF16),
            pltpu.VMEM((DSTATE, TOK), BF16),
            pltpu.VMEM((K, *tile), BF16),
            pltpu.VMEM((K, *tile), BF16),
            pltpu.VMEM((K, *tile), BF16),
            pltpu.VMEM((K // 2, *tile), BF16),
            pltpu.VMEM((K, *tile), BF16),
            pltpu.VMEM((K, *tile), BF16),
            pltpu.VMEM((K // 2, *tile), BF16),
            share,
            share,
            pltpu.VMEM((Z * 8, 128), F32),
            small,
            pltpu.VMEM((K, 128), F32),
            pltpu.VMEM((K, 128), F32),
            pltpu.VMEM((K, 128), F32),
            small,
            dma((XBLOCKS,)), dma, dma((K,)), dma((K,)), dma((K // 2,)),
            dma, dma, dma, dma((TURNS,)), dma, dma, dma, dma, dma,
        ],
        compiler_params=pltpu.CompilerParams(
            vmem_limit_bytes=VMEM_LIMIT, has_side_effects=True, collective_id=0
        ),
        name="layer",
    )(x, b, c, dt, bias, alog, skip)


def on_device(inputs, b_panel, c_panel, dt_raw, dt_bias, a_log, d_skip):
    return layer_call(inputs, b_panel, c_panel, dt_raw, dt_bias[None], a_log[None], d_skip[None])


def solution(mesh):
    return jax.shard_map(
        on_device,
        mesh=mesh,
        in_specs=(P(("seq", "head"), None),) * 4 + (P(), P(), P()),
        out_specs=P(("seq", "head"), None),
        check_vma=False,
    )
```

```python
import functools

import jax
import jax.numpy as jnp
from jax import lax
from jax.experimental import pallas as pl
from jax.experimental.pallas import tpu as pltpu
from jax.sharding import PartitionSpec as P

HEADS = 128
HDIM = 64
DSTATE = 128
TOK = 320
PIECES = HEADS // 2
PARTS = 4
TURNS = 4
XBLOCKS = 8
BATCH = 4
FILL = 24
MEET = 5
LOG2E = 1.4426950408889634
F32 = jnp.float32
BF16 = jnp.bfloat16
VMEM_LIMIT = 56 * 1024 * 1024


def layer_kernel(cfg, x_hbm, b_ref, c_ref, dt_ref, bias_ref, alog_ref, skip_ref, o_ref,
                 x_ref, part_ref, fade_ref, a_ref, rt_ref, sm_ref, g_ref, bt_ref,
                 l_ref, fl, fr, fe, sl, sr, rs, rbuf, eb, za, pa, dec_own, dec_pre, dec_suf, rowdec,
                 x_sem, fl_sem, fr_sem, fe_sem, left_sem, right_sem, rs_sem, rbuf_sem, eb_sem,
                 z_send, z_recv, p_send, p_recv):
    Z, Y, R, K, A, AO, B, C = cfg
    low = Z // 2 - 1
    seq = lax.axis_index("seq")
    head = lax.axis_index("head")
    y = head // Z
    z = head - y * Z
    r = seq * Y + y
    in_plane = (z == low) | (z == low + 1)
    groups = R // PARTS
    part = r // groups
    rest = lax.rem(r, groups)
    diagonal = groups % Y == 0
    group = rest // Y * Y + lax.rem(rest - part + PARTS * Y, Y) if diagonal else rest
    rows = DSTATE // PARTS

    def owner(g, p):
        return p * groups + (g // Y * Y + lax.rem(p + g, Y) if diagonal else g)

    def remote(src, dst, send, recv, to_seq, to_head):
        return pltpu.make_async_remote_copy(
            src_ref=src, dst_ref=dst, send_sem=send, recv_sem=recv,
            device_id={"seq": to_seq, "head": to_head}, device_id_type=pl.DeviceIdType.MESH,
        )

    def await_bytes(ref, sem):
        pltpu.make_async_copy(ref, ref, sem).wait()

    def send_left(src, q):
        remote(src, fr.at[q], left_sem, fr_sem.at[q], seq, head - 1).start()

    def send_right(src, q):
        remote(src, fl.at[q], right_sem, fl_sem.at[q], seq, head + 1).start()

    gate = pltpu.get_barrier_semaphore()

    def greet(to_seq, to_head):
        pl.semaphore_signal(
            gate, inc=1, device_id={"seq": to_seq, "head": to_head}, device_id_type=pl.DeviceIdType.MESH
        )

    for dz in range(1, Z):
        greet(seq, y * Z + lax.rem(z + dz, Z))

    @pl.when(in_plane)
    def _():
        def hello(d, carry):
            to = lax.rem(r + d, R)
            to_seq = to // Y
            greet(to_seq, (to - to_seq * Y) * Z + z)
            return carry

        lax.fori_loop(1, R, hello, 0)

    blocks = XBLOCKS
    width = K * 128 // blocks

    def x_copy(n):
        cols = pl.ds(pl.multiple_of(n * width, width), width)
        return pltpu.make_async_copy(x_hbm.at[:, cols], x_ref.at[:, cols], x_sem.at[n])

    for n in range(blocks):
        x_copy(n).start()

    v = dt_ref[...].astype(F32) + bias_ref[...]
    delta = jnp.maximum(v, 0.0) + jnp.log(1.0 + jnp.exp(-jnp.abs(v)))
    rates = (-LOG2E) * jnp.exp(alog_ref[...]) * delta
    t_at = lax.broadcasted_iota(jnp.int32, (TOK, TOK), 0)
    s_at = lax.broadcasted_iota(jnp.int32, (TOK, TOK), 1)
    lower = (t_at >= s_at).astype(F32)
    a = jnp.dot(lower, rates, precision=lax.Precision.HIGHEST, preferred_element_type=F32)
    a_ref[...] = a
    g_ref[...] = (jnp.exp2(a[TOK - 1 : TOK, :] - a) * delta).astype(BF16)
    bt_ref[...] = b_ref[...].astype(F32).T.astype(BF16)

    piece_at = lax.broadcasted_iota(jnp.int32, (K, 128), 0)
    head_at = lax.broadcasted_iota(jnp.int32, (K, 128), 1)
    pick_head = lax.broadcasted_iota(jnp.int32, (128, 128), 0)
    pick_lane = lax.broadcasted_iota(jnp.int32, (128, 128), 1) // HDIM

    def per_piece(value):
        second = (lax.rem(pick_head, 2) == pick_lane).astype(F32)
        only = jnp.where(head_at // 2 == piece_at, value, 0.0)
        logs = jnp.dot(only, second, precision=lax.Precision.HIGHEST, preferred_element_type=F32)
        return jnp.exp2(logs)

    dec_own[...] = per_piece(a[TOK - 1 : TOK, :])
    my_row = pl.ds(pl.multiple_of(z * 8, 8), 8)
    za[my_row, :] = jnp.broadcast_to(a[TOK - 1 : TOK, :], (8, 128))

    pl.semaphore_wait(gate, Z - 1 + jnp.where(in_plane, R - 1, 0))

    for dz in range(1, Z):
        remote(za.at[my_row, :], za.at[my_row, :], z_send, z_recv, seq, y * Z + lax.rem(z + dz, Z)).start()

    def meet_row():
        await_bytes(za.at[0 : 8 * (Z - 1), :], z_recv)
        before = jnp.zeros((8, 128), F32)
        after = jnp.zeros((8, 128), F32)
        for other in range(Z):
            value = za[8 * other : 8 * other + 8, :]
            before = before + jnp.where(other < z, value, 0.0)
            after = after + jnp.where(other > z, value, 0.0)
        total = before + after + za[my_row, :]

        @pl.when(in_plane)
        def _():
            slot = pl.ds(pl.multiple_of(r * 8, 8), 8)
            pa[slot, :] = total

            def tell(d, carry):
                to = lax.rem(r + d, R)
                to_seq = to // Y
                remote(
                    pa.at[slot, :], pa.at[slot, :], p_send, p_recv, to_seq, (to - to_seq * Y) * Z + z
                ).start()
                return carry

            lax.fori_loop(1, R, tell, 0)

        dec_pre[...] = per_piece(before[0:1, :])
        dec_suf[...] = per_piece(after[0:1, :])

    def score_tables():
        v = dt_ref[...].astype(F32) + bias_ref[...]
        delta = jnp.maximum(v, 0.0) + jnp.log(1.0 + jnp.exp(-jnp.abs(v)))
        rt_ref[...] = (a_ref[...] - jnp.log2(delta)).T
        scores = lax.dot_general(c_ref[...], b_ref[...], (((1,), (1,)), ((), ())), preferred_element_type=F32)
        t_at = lax.broadcasted_iota(jnp.int32, (TOK, TOK), 0)
        s_at = lax.broadcasted_iota(jnp.int32, (TOK, TOK), 1)
        sm_ref[...] = jnp.where(t_at >= s_at, scores, 0.0)

    lane = lax.broadcasted_iota(jnp.int32, (TOK, 128), 1)
    first = lane < HDIM

    def columns_of(q):
        return pl.ds(pl.multiple_of(q * 128, 128), 128)

    wide_head = lax.broadcasted_iota(jnp.int32, (128, 128 * BATCH), 0)
    wide_lane = lax.broadcasted_iota(jnp.int32, (128, 128 * BATCH), 1) // HDIM

    def local_states(q):
        cols = pl.ds(pl.multiple_of(q * 128, 128 * BATCH), 128 * BATCH)
        spread = (wide_head == 2 * q + wide_lane).astype(BF16)
        gain = jnp.dot(g_ref[...], spread, preferred_element_type=F32)
        scaled = (x_ref[:, cols].astype(F32) * gain).astype(BF16)
        state = jnp.dot(bt_ref[...], scaled, preferred_element_type=F32).astype(BF16)
        for u in range(BATCH):
            l_ref[q + u] = state[:, 128 * u : 128 * (u + 1)]

    def within_and_skip(start):
        turned = pltpu.roll(a_ref[...], lax.rem(HEADS - 2 * start, HEADS), 1)
        for u in range(2):
            q = start + u
            x = x_ref[:, columns_of(q)]
            columns, parts = [], []
            for k in range(2):
                h = 2 * u + k
                column = jnp.broadcast_to(turned[:, h : h + 1], (TOK, 128))
                columns.append(column)
                row = rt_ref[pl.ds(2 * q + k, 1), :]
                outs = []
                for t0, t1 in ((0, 128), (128, 256), (256, TOK)):
                    tiles = []
                    for s0 in range(0, t1, 128):
                        s1 = min(s0 + 128, t1)
                        gap = column[t0:t1, : s1 - s0] - row[:, s0:s1]
                        if s1 > t0:
                            gap = jnp.minimum(gap, 100.0)
                        tiles.append((sm_ref[t0:t1, s0:s1] * jnp.exp2(gap)).astype(BF16))
                    w = jnp.concatenate(tiles, axis=1) if len(tiles) > 1 else tiles[0]
                    outs.append(jnp.dot(w, x[:t1], preferred_element_type=F32))
                parts.append(jnp.concatenate(outs, axis=0))
            fade_ref[q] = jnp.exp2(jnp.where(first, columns[0], columns[1]))
            skip = jnp.where(first, skip_ref[0, 2 * q], skip_ref[0, 2 * q + 1])
            part_ref[q] = jnp.where(first, parts[0], parts[1]) + skip * x.astype(F32)

    def finish(start):
        both = jnp.concatenate([fl[start], fl[start + 1]], axis=1)
        carried = jnp.dot(c_ref[...], both, preferred_element_type=F32)
        for u in range(2):
            q = start + u
            here = part_ref[q] + fade_ref[q] * carried[:, 128 * u : 128 * (u + 1)]
            o_ref[:, columns_of(q)] = here.astype(BF16)

    def tick(i, carry):
        @pl.when(i == MEET)
        def _():
            meet_row()

        for par in range(2):
            m = low + par
            q = i - (4 * A + B + C) - AO * jnp.abs(z - m)
            at = jnp.clip(q, 0, K - 1)
            k = at // 2
            valid = (q >= 0) & (q < K) & (lax.rem(at, 2) == par)

            @pl.when(valid & (z < m))
            def _():
                remote(sl.at[at], fr.at[at], left_sem, fr_sem.at[at], seq, head + 1).wait_recv()

                @pl.when(z > 0)
                def _():
                    send_left(fr.at[at], at)
                    fl[at] = (fl[at].astype(F32) + dec_pre[pl.ds(at, 1), :] * fr[at].astype(F32)).astype(BF16)

                @pl.when(z == 0)
                def _():
                    fl[at] = fr[at]

            @pl.when(valid & (z == m))
            def _():
                mine = group == lax.rem(k, groups)

                @pl.when(mine)
                def _():
                    await_bytes(fe.at[k, 0 : rows * (PARTS - 1)], fe_sem.at[k])

                @pl.when(jnp.logical_not(mine))
                def _():
                    await_bytes(fe.at[k], fe_sem.at[k])

                send_left(fe.at[k], at)
                entering = fl[at].astype(F32) + dec_pre[pl.ds(at, 1), :] * fe[k].astype(F32)
                fl[at] = entering.astype(BF16)
                sr[at] = (dec_own[pl.ds(at, 1), :] * entering + l_ref[at].astype(F32)).astype(BF16)
                send_right(sr.at[at], at)

            @pl.when(valid & (z > m))
            def _():
                remote(sr.at[at], fl.at[at], right_sem, fl_sem.at[at], seq, head - 1).wait_recv()

                @pl.when(z < Z - 1)
                def _():
                    sr[at] = (dec_own[pl.ds(at, 1), :] * fl[at].astype(F32) + l_ref[at].astype(F32)).astype(BF16)
                    send_right(sr.at[at], at)

        ahead = jnp.minimum(i, K - 1)
        per_block = K // XBLOCKS

        @pl.when((i < K) & (lax.rem(ahead, per_block) == 0))
        def _():
            x_copy(ahead // per_block).wait()

        @pl.when((i < K) & (lax.rem(ahead, BATCH) == 0))
        def _():
            local_states(pl.multiple_of(ahead, BATCH))

        q = i - A * z
        at = jnp.clip(q, 0, K - 1)
        valid = (q >= 0) & (q < K) & (z < low + lax.rem(at, 2))

        @pl.when(valid & (z == 0))
        def _():
            send_right(l_ref.at[at], at)

        @pl.when(valid & (z > 0))
        def _():
            remote(sr.at[at], fl.at[at], right_sem, fl_sem.at[at], seq, head - 1).wait_recv()
            sr[at] = (dec_own[pl.ds(at, 1), :] * fl[at].astype(F32) + l_ref[at].astype(F32)).astype(BF16)
            send_right(sr.at[at], at)

        q1 = i - A * (Z - 1 - z)
        at1 = jnp.clip(q1, 0, K - 1)
        valid1 = (q1 >= 0) & (q1 < K) & (z > low + lax.rem(at1, 2))

        @pl.when(valid1 & (z == Z - 1))
        def _():
            send_left(l_ref.at[at1], at1)

        @pl.when(valid1 & (z < Z - 1))
        def _():
            remote(sl.at[at1], fr.at[at1], left_sem, fr_sem.at[at1], seq, head + 1).wait_recv()
            sl[at1] = (dec_suf[pl.ds(at1, 1), :] * l_ref[at1].astype(F32) + fr[at1].astype(F32)).astype(BF16)
            send_left(sl.at[at1], at1)

        q2 = i - 4 * A
        at2 = jnp.clip(q2, 0, K - 1)
        k2 = at2 // 2

        @pl.when((q2 >= 0) & (q2 < K) & (z == low + lax.rem(at2, 2)))
        def _():
            remote(sr.at[at2], fl.at[at2], right_sem, fl_sem.at[at2], seq, head - 1).wait_recv()
            remote(sl.at[at2], fr.at[at2], left_sem, fr_sem.at[at2], seq, head + 1).wait_recv()
            inner = dec_own[pl.ds(at2, 1), :] * fl[at2].astype(F32) + l_ref[at2].astype(F32)
            total = (dec_suf[pl.ds(at2, 1), :] * inner + fr[at2].astype(F32)).astype(BF16)

            rs[k2] = total
            turn = k2 // groups
            for p in range(PARTS):
                to = owner(lax.rem(k2, groups), p)

                @pl.when(to == r)
                def _():
                    rbuf[turn, r] = total[rows * p : rows * (p + 1)]

                @pl.when(to != r)
                def _():
                    to_seq = to // Y
                    remote(
                        rs.at[k2, rows * p : rows * (p + 1)], rbuf.at[turn, r], rs_sem, rbuf_sem.at[turn],
                        to_seq, (to - to_seq * Y) * Z + z,
                    ).start()

        @pl.when(in_plane & (i == 4 * A))
        def _():
            await_bytes(pa.at[0 : 8 * (R - 1), :], p_recv)

        for turn in range(TURNS):
            k3 = group + turn * groups
            q3 = 2 * k3 + (z - low)

            @pl.when(in_plane & (i == q3 + 4 * A + B))
            def _():
                chosen = (pick_head == 2 * q3 + pick_lane).astype(F32)
                rowdec[...] = jnp.exp2(
                    jnp.dot(pa[...], chosen, precision=lax.Precision.HIGHEST, preferred_element_type=F32)
                )
                await_bytes(rbuf.at[turn, 0 : R - 1], rbuf_sem.at[turn])
                span = pl.ds(pl.multiple_of(part * rows, rows), rows)

                def row(s, run):
                    e = run.astype(BF16)

                    @pl.when(s == r)
                    def _():
                        fe[k3, span] = e

                    @pl.when(s != r)
                    def _():
                        eb[turn, s] = e
                        to_seq = s // Y
                        remote(
                            eb.at[turn, s], fe.at[k3, span], eb_sem, fe_sem.at[k3],
                            to_seq, (s - to_seq * Y) * Z + z,
                        ).start()

                    return rowdec[pl.ds(s * 8, 1), :] * run + rbuf[turn, s].astype(F32)

                lax.fori_loop(0, R, row, jnp.zeros((rows, 128), F32))

        @pl.when(i == 0)
        def _():
            score_tables()

        early = FILL // 2
        w = jnp.where(i < FILL, i // 2, early + (i - FILL) // 4)
        now = jnp.where(i < FILL, lax.rem(i, 2) == 0, lax.rem(i, 4) == 0)
        w_at = jnp.minimum(w, K // 2 - 1)

        @pl.when(now & (w < K // 2))
        def _():
            within_and_skip(2 * w_at)

        far = jnp.maximum(jnp.abs(z - low), jnp.abs(z - low - 1))
        done = i - (4 * A + B + C) - AO * far - 1
        done_at = jnp.clip(done, 0, K - 2)

        @pl.when((done >= 0) & (done < K - 1) & (lax.rem(done_at, 2) == 0))
        def _():
            finish(done_at)

        return carry

    lax.fori_loop(0, K + 4 * A + B + C + AO * (Z // 2), tick, 0)

    await_bytes(za.at[0 : 8 * (Z - 1), :], z_send)

    @pl.when(z > 0)
    def _():
        await_bytes(sl, left_sem)

    @pl.when(z < Z - 1)
    def _():
        await_bytes(sr, right_sem)

    @pl.when(in_plane)
    def _():
        await_bytes(pa.at[0 : 8 * (R - 1), :], p_send)
        for turn in range(TURNS):
            await_bytes(rbuf.at[turn, 0 : R - 1], rs_sem)
            await_bytes(rbuf.at[turn, 0 : R - 1], eb_sem)


def layer_call(x, b, c, dt, bias, alog, skip, Z=8, K=PIECES, A=6, AO=6, B=8, C=10):
    Y = lax.axis_size("head") // Z
    R = lax.axis_size("seq") * Y
    tile = (DSTATE, 128)
    dma = pltpu.SemaphoreType.DMA
    vmem = pl.BlockSpec(memory_space=pltpu.VMEM)
    hbm = pl.BlockSpec(memory_space=pl.ANY)
    small = pltpu.VMEM((R * 8, 128), F32)
    share = pltpu.VMEM((TURNS, R, DSTATE // PARTS, 128), BF16)
    return pl.pallas_call(
        functools.partial(layer_kernel, (Z, Y, R, K, A, AO, B, C)),
        in_specs=[hbm, vmem, vmem, vmem, vmem, vmem, pl.BlockSpec(memory_space=pltpu.SMEM)],
        out_specs=vmem,
        out_shape=pltpu.VMEM((TOK, K * 128), BF16) if K == PIECES else jax.ShapeDtypeStruct((TOK, K * 128), BF16),
        scratch_shapes=[
            pltpu.VMEM((TOK, K * 128), BF16),
            pltpu.VMEM((K, TOK, 128), F32),
            pltpu.VMEM((K, TOK, 128), F32),
            pltpu.VMEM((TOK, HEADS), F32),
            pltpu.VMEM((HEADS, TOK), F32),
            pltpu.VMEM((TOK, TOK), F32),
            pltpu.VMEM((TOK, HEADS), BF16),
            pltpu.VMEM((DSTATE, TOK), BF16),
            pltpu.VMEM((K, *tile), BF16),
            pltpu.VMEM((K, *tile), BF16),
            pltpu.VMEM((K, *tile), BF16),
            pltpu.VMEM((K // 2, *tile), BF16),
            pltpu.VMEM((K, *tile), BF16),
            pltpu.VMEM((K, *tile), BF16),
            pltpu.VMEM((K // 2, *tile), BF16),
            share,
            share,
            pltpu.VMEM((Z * 8, 128), F32),
            small,
            pltpu.VMEM((K, 128), F32),
            pltpu.VMEM((K, 128), F32),
            pltpu.VMEM((K, 128), F32),
            small,
            dma((XBLOCKS,)), dma((K,)), dma((K,)), dma((K // 2,)),
            dma, dma, dma, dma((TURNS,)), dma, dma, dma, dma, dma,
        ],
        compiler_params=pltpu.CompilerParams(
            vmem_limit_bytes=VMEM_LIMIT, has_side_effects=True, collective_id=0
        ),
        name="layer",
    )(x, b, c, dt, bias, alog, skip)


def store_kernel(y_ref, o_hbm, sem):
    copy = pltpu.make_async_copy(y_ref, o_hbm, sem)
    copy.start()
    copy.wait()


def store_call(y):
    return pl.pallas_call(
        store_kernel,
        in_specs=[pl.BlockSpec(memory_space=pltpu.VMEM)],
        out_specs=pl.BlockSpec(memory_space=pl.ANY),
        out_shape=jax.ShapeDtypeStruct(y.shape, y.dtype),
        scratch_shapes=[pltpu.SemaphoreType.DMA],
        compiler_params=pltpu.CompilerParams(vmem_limit_bytes=8 * 1024 * 1024),
        name="store",
    )(y)


def on_device(inputs, b_panel, c_panel, dt_raw, dt_bias, a_log, d_skip):
    y = layer_call(inputs, b_panel, c_panel, dt_raw, dt_bias[None], a_log[None], d_skip[None])
    return store_call(y)


def solution(mesh):
    return jax.shard_map(
        on_device,
        mesh=mesh,
        in_specs=(P(("seq", "head"), None),) * 4 + (P(), P(), P()),
        out_specs=P(("seq", "head"), None),
        check_vma=False,
    )
```

```python
import functools

import jax
import jax.numpy as jnp
from jax import lax
from jax.experimental import pallas as pl
from jax.experimental.pallas import tpu as pltpu
from jax.sharding import PartitionSpec as P

HEADS = 128
HDIM = 64
DSTATE = 128
TOK = 320
PIECES = HEADS // 2
PARTS = 4
TURNS = 4
XBLOCKS = 8
BATCH = 4
FILL = 24
MEET = 5
STORES = 4
LOG2E = 1.4426950408889634
F32 = jnp.float32
BF16 = jnp.bfloat16
VMEM_LIMIT = 56 * 1024 * 1024


def layer_kernel(cfg, x_hbm, b_hbm, c_hbm, dt_hbm, bias_hbm, alog_hbm, skip_hbm, o_ref,
                 b_ref, c_ref, dt_ref, bias_ref, alog_ref, skip_ref, skips,
                 x_ref, part_ref, fade_ref, a_ref, rt_ref, sm_ref, g_ref, bt_ref,
                 l_ref, fl, fr, fe, sl, sr, rs, rbuf, eb, za, pa, dec_own, dec_pre, dec_suf, rowdec,
                 in_sem, x_sem, fl_sem, fr_sem, fe_sem, left_sem, right_sem, rs_sem, rbuf_sem, eb_sem,
                 z_send, z_recv, p_send, p_recv):
    Z, Y, R, K, A, AO, B, C = cfg
    low = Z // 2 - 1
    seq = lax.axis_index("seq")
    head = lax.axis_index("head")
    y = head // Z
    z = head - y * Z
    r = seq * Y + y
    in_plane = (z == low) | (z == low + 1)
    groups = R // PARTS
    part = r // groups
    rest = lax.rem(r, groups)
    diagonal = groups % Y == 0
    group = rest // Y * Y + lax.rem(rest - part + PARTS * Y, Y) if diagonal else rest
    rows = DSTATE // PARTS

    def owner(g, p):
        return p * groups + (g // Y * Y + lax.rem(p + g, Y) if diagonal else g)

    def remote(src, dst, send, recv, to_seq, to_head):
        return pltpu.make_async_remote_copy(
            src_ref=src, dst_ref=dst, send_sem=send, recv_sem=recv,
            device_id={"seq": to_seq, "head": to_head}, device_id_type=pl.DeviceIdType.MESH,
        )

    def await_bytes(ref, sem):
        pltpu.make_async_copy(ref, ref, sem).wait()

    def send_left(src, q):
        remote(src, fr.at[q], left_sem, fr_sem.at[q], seq, head - 1).start()

    def send_right(src, q):
        remote(src, fl.at[q], right_sem, fl_sem.at[q], seq, head + 1).start()

    pairs = ((b_hbm, b_ref), (c_hbm, c_ref), (dt_hbm, dt_ref), (bias_hbm, bias_ref), (alog_hbm, alog_ref), (skip_hbm, skip_ref))
    loads = [pltpu.make_async_copy(src, dst, in_sem.at[n]) for n, (src, dst) in enumerate(pairs)]
    for copy in loads:
        copy.start()

    gate = pltpu.get_barrier_semaphore()

    def greet(to_seq, to_head):
        pl.semaphore_signal(
            gate, inc=1, device_id={"seq": to_seq, "head": to_head}, device_id_type=pl.DeviceIdType.MESH
        )

    for dz in range(1, Z):
        greet(seq, y * Z + lax.rem(z + dz, Z))

    @pl.when(in_plane)
    def _():
        def hello(d, carry):
            to = lax.rem(r + d, R)
            to_seq = to // Y
            greet(to_seq, (to - to_seq * Y) * Z + z)
            return carry

        lax.fori_loop(1, R, hello, 0)

    blocks = XBLOCKS
    width = K * 128 // blocks

    def x_copy(n):
        cols = pl.ds(pl.multiple_of(n * width, width), width)
        return pltpu.make_async_copy(x_hbm.at[:, cols], x_ref.at[:, cols], x_sem.at[n])

    for n in range(blocks):
        x_copy(n).start()

    for copy in loads:
        copy.wait()

    v = dt_ref[...].astype(F32) + bias_ref[...]
    delta = jnp.maximum(v, 0.0) + jnp.log(1.0 + jnp.exp(-jnp.abs(v)))
    rates = (-LOG2E) * jnp.exp(alog_ref[...]) * delta
    t_at = lax.broadcasted_iota(jnp.int32, (TOK, TOK), 0)
    s_at = lax.broadcasted_iota(jnp.int32, (TOK, TOK), 1)
    lower = (t_at >= s_at).astype(F32)
    a = jnp.dot(lower, rates, precision=lax.Precision.HIGHEST, preferred_element_type=F32)
    a_ref[...] = a
    g_ref[...] = (jnp.exp2(a[TOK - 1 : TOK, :] - a) * delta).astype(BF16)
    bt_ref[...] = b_ref[...].astype(F32).T.astype(BF16)

    piece_at = lax.broadcasted_iota(jnp.int32, (K, 128), 0)
    head_at = lax.broadcasted_iota(jnp.int32, (K, 128), 1)
    pick_head = lax.broadcasted_iota(jnp.int32, (128, 128), 0)
    pick_lane = lax.broadcasted_iota(jnp.int32, (128, 128), 1) // HDIM

    def per_piece(value):
        second = (lax.rem(pick_head, 2) == pick_lane).astype(F32)
        only = jnp.where(head_at // 2 == piece_at, value, 0.0)
        logs = jnp.dot(only, second, precision=lax.Precision.HIGHEST, preferred_element_type=F32)
        return logs

    dec_own[...] = jnp.exp2(per_piece(a[TOK - 1 : TOK, :]))
    my_row = pl.ds(pl.multiple_of(z * 8, 8), 8)
    za[my_row, :] = jnp.broadcast_to(a[TOK - 1 : TOK, :], (8, 128))

    pl.semaphore_wait(gate, Z - 1 + jnp.where(in_plane, R - 1, 0))

    for dz in range(1, Z):
        remote(za.at[my_row, :], za.at[my_row, :], z_send, z_recv, seq, y * Z + lax.rem(z + dz, Z)).start()

    def meet_row():
        await_bytes(za.at[0 : 8 * (Z - 1), :], z_recv)
        before = jnp.zeros((8, 128), F32)
        after = jnp.zeros((8, 128), F32)
        for other in range(Z):
            value = za[8 * other : 8 * other + 8, :]
            before = before + jnp.where(other < z, value, 0.0)
            after = after + jnp.where(other > z, value, 0.0)
        total = before + after + za[my_row, :]

        @pl.when(in_plane)
        def _():
            slot = pl.ds(pl.multiple_of(r * 8, 8), 8)
            pa[slot, :] = total

            def tell(d, carry):
                to = lax.rem(r + d, R)
                to_seq = to // Y
                remote(
                    pa.at[slot, :], pa.at[slot, :], p_send, p_recv, to_seq, (to - to_seq * Y) * Z + z
                ).start()
                return carry

            lax.fori_loop(1, R, tell, 0)

        dec_pre[...] = jnp.exp2(per_piece(before[0:1, :]))
        dec_suf[...] = jnp.exp2(per_piece(after[0:1, :]))

    def score_tables():
        v = dt_ref[...].astype(F32) + bias_ref[...]
        delta = jnp.maximum(v, 0.0) + jnp.log(1.0 + jnp.exp(-jnp.abs(v)))
        rt_ref[...] = (a_ref[...] - jnp.log2(delta)).T
        scores = lax.dot_general(c_ref[...], b_ref[...], (((1,), (1,)), ((), ())), preferred_element_type=F32)
        t_at = lax.broadcasted_iota(jnp.int32, (TOK, TOK), 0)
        s_at = lax.broadcasted_iota(jnp.int32, (TOK, TOK), 1)
        sm_ref[...] = jnp.where(t_at >= s_at, scores, 0.0)
        skips[...] = per_piece(skip_ref[...])

    lane = lax.broadcasted_iota(jnp.int32, (TOK, 128), 1)
    first = lane < HDIM

    def columns_of(q):
        return pl.ds(pl.multiple_of(q * 128, 128), 128)

    wide_head = lax.broadcasted_iota(jnp.int32, (128, 128 * BATCH), 0)
    wide_lane = lax.broadcasted_iota(jnp.int32, (128, 128 * BATCH), 1) // HDIM

    def local_states(q):
        cols = pl.ds(pl.multiple_of(q * 128, 128 * BATCH), 128 * BATCH)
        spread = (wide_head == 2 * q + wide_lane).astype(BF16)
        gain = jnp.dot(g_ref[...], spread, preferred_element_type=F32)
        scaled = (x_ref[:, cols].astype(F32) * gain).astype(BF16)
        state = jnp.dot(bt_ref[...], scaled, preferred_element_type=F32).astype(BF16)
        for u in range(BATCH):
            l_ref[q + u] = state[:, 128 * u : 128 * (u + 1)]

    def within_and_skip(start):
        turned = pltpu.roll(a_ref[...], lax.rem(HEADS - 2 * start, HEADS), 1)
        for u in range(2):
            q = start + u
            x = x_ref[:, columns_of(q)]
            columns, parts = [], []
            for k in range(2):
                h = 2 * u + k
                column = jnp.broadcast_to(turned[:, h : h + 1], (TOK, 128))
                columns.append(column)
                row = rt_ref[pl.ds(2 * q + k, 1), :]
                outs = []
                for t0, t1 in ((0, 128), (128, 256), (256, TOK)):
                    tiles = []
                    for s0 in range(0, t1, 128):
                        s1 = min(s0 + 128, t1)
                        gap = column[t0:t1, : s1 - s0] - row[:, s0:s1]
                        if s1 > t0:
                            gap = jnp.minimum(gap, 100.0)
                        tiles.append((sm_ref[t0:t1, s0:s1] * jnp.exp2(gap)).astype(BF16))
                    w = jnp.concatenate(tiles, axis=1) if len(tiles) > 1 else tiles[0]
                    outs.append(jnp.dot(w, x[:t1], preferred_element_type=F32))
                parts.append(jnp.concatenate(outs, axis=0))
            fade_ref[q] = jnp.exp2(jnp.where(first, columns[0], columns[1]))
            part_ref[q] = jnp.where(first, parts[0], parts[1]) + skips[pl.ds(q, 1), :] * x.astype(F32)

    def finish(start):
        both = jnp.concatenate([fl[start], fl[start + 1]], axis=1)
        carried = jnp.dot(c_ref[...], both, preferred_element_type=F32)
        for u in range(2):
            q = start + u
            here = part_ref[q] + fade_ref[q] * carried[:, 128 * u : 128 * (u + 1)]
            o_ref[:, columns_of(q)] = here.astype(BF16)

    def tick(i, carry):
        @pl.when(i == MEET)
        def _():
            meet_row()

        for par in range(2):
            m = low + par
            q = i - (4 * A + B + C) - AO * jnp.abs(z - m)
            at = jnp.clip(q, 0, K - 1)
            k = at // 2
            valid = (q >= 0) & (q < K) & (lax.rem(at, 2) == par)

            @pl.when(valid & (z < m))
            def _():
                remote(sl.at[at], fr.at[at], left_sem, fr_sem.at[at], seq, head + 1).wait_recv()

                @pl.when(z > 0)
                def _():
                    send_left(fr.at[at], at)
                    fl[at] = (fl[at].astype(F32) + dec_pre[pl.ds(at, 1), :] * fr[at].astype(F32)).astype(BF16)

                @pl.when(z == 0)
                def _():
                    fl[at] = fr[at]

            @pl.when(valid & (z == m))
            def _():
                mine = group == lax.rem(k, groups)

                @pl.when(mine)
                def _():
                    await_bytes(fe.at[k, 0 : rows * (PARTS - 1)], fe_sem.at[k])

                @pl.when(jnp.logical_not(mine))
                def _():
                    await_bytes(fe.at[k], fe_sem.at[k])

                send_left(fe.at[k], at)
                entering = fl[at].astype(F32) + dec_pre[pl.ds(at, 1), :] * fe[k].astype(F32)
                fl[at] = entering.astype(BF16)
                sr[at] = (dec_own[pl.ds(at, 1), :] * entering + l_ref[at].astype(F32)).astype(BF16)
                send_right(sr.at[at], at)

            @pl.when(valid & (z > m))
            def _():
                remote(sr.at[at], fl.at[at], right_sem, fl_sem.at[at], seq, head - 1).wait_recv()

                @pl.when(z < Z - 1)
                def _():
                    sr[at] = (dec_own[pl.ds(at, 1), :] * fl[at].astype(F32) + l_ref[at].astype(F32)).astype(BF16)
                    send_right(sr.at[at], at)

        ahead = jnp.minimum(i, K - 1)
        per_block = K // XBLOCKS

        @pl.when((i < K) & (lax.rem(ahead, per_block) == 0))
        def _():
            x_copy(ahead // per_block).wait()

        @pl.when((i < K) & (lax.rem(ahead, BATCH) == 0))
        def _():
            local_states(pl.multiple_of(ahead, BATCH))

        q = i - A * z
        at = jnp.clip(q, 0, K - 1)
        valid = (q >= 0) & (q < K) & (z < low + lax.rem(at, 2))

        @pl.when(valid & (z == 0))
        def _():
            send_right(l_ref.at[at], at)

        @pl.when(valid & (z > 0))
        def _():
            remote(sr.at[at], fl.at[at], right_sem, fl_sem.at[at], seq, head - 1).wait_recv()
            sr[at] = (dec_own[pl.ds(at, 1), :] * fl[at].astype(F32) + l_ref[at].astype(F32)).astype(BF16)
            send_right(sr.at[at], at)

        q1 = i - A * (Z - 1 - z)
        at1 = jnp.clip(q1, 0, K - 1)
        valid1 = (q1 >= 0) & (q1 < K) & (z > low + lax.rem(at1, 2))

        @pl.when(valid1 & (z == Z - 1))
        def _():
            send_left(l_ref.at[at1], at1)

        @pl.when(valid1 & (z < Z - 1))
        def _():
            remote(sl.at[at1], fr.at[at1], left_sem, fr_sem.at[at1], seq, head + 1).wait_recv()
            sl[at1] = (dec_suf[pl.ds(at1, 1), :] * l_ref[at1].astype(F32) + fr[at1].astype(F32)).astype(BF16)
            send_left(sl.at[at1], at1)

        q2 = i - 4 * A
        at2 = jnp.clip(q2, 0, K - 1)
        k2 = at2 // 2

        @pl.when((q2 >= 0) & (q2 < K) & (z == low + lax.rem(at2, 2)))
        def _():
            remote(sr.at[at2], fl.at[at2], right_sem, fl_sem.at[at2], seq, head - 1).wait_recv()
            remote(sl.at[at2], fr.at[at2], left_sem, fr_sem.at[at2], seq, head + 1).wait_recv()
            inner = dec_own[pl.ds(at2, 1), :] * fl[at2].astype(F32) + l_ref[at2].astype(F32)
            total = (dec_suf[pl.ds(at2, 1), :] * inner + fr[at2].astype(F32)).astype(BF16)

            rs[k2] = total
            turn = k2 // groups
            for p in range(PARTS):
                to = owner(lax.rem(k2, groups), p)

                @pl.when(to == r)
                def _():
                    rbuf[turn, r] = total[rows * p : rows * (p + 1)]

                @pl.when(to != r)
                def _():
                    to_seq = to // Y
                    remote(
                        rs.at[k2, rows * p : rows * (p + 1)], rbuf.at[turn, r], rs_sem, rbuf_sem.at[turn],
                        to_seq, (to - to_seq * Y) * Z + z,
                    ).start()

        @pl.when(in_plane & (i == 4 * A))
        def _():
            await_bytes(pa.at[0 : 8 * (R - 1), :], p_recv)

        for turn in range(TURNS):
            k3 = group + turn * groups
            q3 = 2 * k3 + (z - low)

            @pl.when(in_plane & (i == q3 + 4 * A + B))
            def _():
                chosen = (pick_head == 2 * q3 + pick_lane).astype(F32)
                rowdec[...] = jnp.exp2(
                    jnp.dot(pa[...], chosen, precision=lax.Precision.HIGHEST, preferred_element_type=F32)
                )
                await_bytes(rbuf.at[turn, 0 : R - 1], rbuf_sem.at[turn])
                span = pl.ds(pl.multiple_of(part * rows, rows), rows)

                def row(s, run):
                    e = run.astype(BF16)

                    @pl.when(s == r)
                    def _():
                        fe[k3, span] = e

                    @pl.when(s != r)
                    def _():
                        eb[turn, s] = e
                        to_seq = s // Y
                        remote(
                            eb.at[turn, s], fe.at[k3, span], eb_sem, fe_sem.at[k3],
                            to_seq, (s - to_seq * Y) * Z + z,
                        ).start()

                    return rowdec[pl.ds(s * 8, 1), :] * run + rbuf[turn, s].astype(F32)

                lax.fori_loop(0, R, row, jnp.zeros((rows, 128), F32))

        @pl.when(i == 0)
        def _():
            score_tables()

        early = FILL // 2
        w = jnp.where(i < FILL, i // 2, early + (i - FILL) // 4)
        now = jnp.where(i < FILL, lax.rem(i, 2) == 0, lax.rem(i, 4) == 0)
        w_at = jnp.minimum(w, K // 2 - 1)

        @pl.when(now & (w < K // 2))
        def _():
            within_and_skip(2 * w_at)

        far = jnp.maximum(jnp.abs(z - low), jnp.abs(z - low - 1))
        done = i - (4 * A + B + C) - AO * far - 1
        done_at = jnp.clip(done, 0, K - 2)

        @pl.when((done >= 0) & (done < K - 1) & (lax.rem(done_at, 2) == 0))
        def _():
            finish(done_at)

        return carry

    lax.fori_loop(0, K + 4 * A + B + C + AO * (Z // 2), tick, 0)

    await_bytes(za.at[0 : 8 * (Z - 1), :], z_send)

    @pl.when(z > 0)
    def _():
        await_bytes(sl, left_sem)

    @pl.when(z < Z - 1)
    def _():
        await_bytes(sr, right_sem)

    @pl.when(in_plane)
    def _():
        await_bytes(pa.at[0 : 8 * (R - 1), :], p_send)
        for turn in range(TURNS):
            await_bytes(rbuf.at[turn, 0 : R - 1], rs_sem)
            await_bytes(rbuf.at[turn, 0 : R - 1], eb_sem)


def layer_call(x, b, c, dt, bias, alog, skip, Z=8, K=PIECES, A=6, AO=6, B=7, C=8):
    Y = lax.axis_size("head") // Z
    R = lax.axis_size("seq") * Y
    tile = (DSTATE, 128)
    dma = pltpu.SemaphoreType.DMA
    vmem = pl.BlockSpec(memory_space=pltpu.VMEM)
    hbm = pl.BlockSpec(memory_space=pl.ANY)
    small = pltpu.VMEM((R * 8, 128), F32)
    share = pltpu.VMEM((TURNS, R, DSTATE // PARTS, 128), BF16)
    return pl.pallas_call(
        functools.partial(layer_kernel, (Z, Y, R, K, A, AO, B, C)),
        in_specs=[hbm] * 7,
        out_specs=vmem,
        out_shape=pltpu.VMEM((TOK, K * 128), BF16) if K == PIECES else jax.ShapeDtypeStruct((TOK, K * 128), BF16),
        scratch_shapes=[
            pltpu.VMEM((TOK, DSTATE), BF16),
            pltpu.VMEM((TOK, DSTATE), BF16),
            pltpu.VMEM((TOK, HEADS), BF16),
            pltpu.VMEM((1, HEADS), F32),
            pltpu.VMEM((1, HEADS), F32),
            pltpu.VMEM((1, HEADS), F32),
            pltpu.VMEM((K, 128), F32),
            pltpu.VMEM((TOK, K * 128), BF16),
            pltpu.VMEM((K, TOK, 128), F32),
            pltpu.VMEM((K, TOK, 128), F32),
            pltpu.VMEM((TOK, HEADS), F32),
            pltpu.VMEM((HEADS, TOK), F32),
            pltpu.VMEM((TOK, TOK), F32),
            pltpu.VMEM((TOK, HEADS), BF16),
            pltpu.VMEM((DSTATE, TOK), BF16),
            pltpu.VMEM((K, *tile), BF16),
            pltpu.VMEM((K, *tile), BF16),
            pltpu.VMEM((K, *tile), BF16),
            pltpu.VMEM((K // 2, *tile), BF16),
            pltpu.VMEM((K, *tile), BF16),
            pltpu.VMEM((K, *tile), BF16),
            pltpu.VMEM((K // 2, *tile), BF16),
            share,
            share,
            pltpu.VMEM((Z * 8, 128), F32),
            small,
            pltpu.VMEM((K, 128), F32),
            pltpu.VMEM((K, 128), F32),
            pltpu.VMEM((K, 128), F32),
            small,
            dma((6,)), dma((XBLOCKS,)), dma((K,)), dma((K,)), dma((K // 2,)),
            dma, dma, dma, dma((TURNS,)), dma, dma, dma, dma, dma,
        ],
        compiler_params=pltpu.CompilerParams(
            vmem_limit_bytes=VMEM_LIMIT, has_side_effects=True, collective_id=0
        ),
        name="layer",
    )(x, b, c, dt, bias, alog, skip)


def store_kernel(y_ref, o_hbm, sem):
    rows = TOK // STORES
    copies = [
        pltpu.make_async_copy(y_ref.at[rows * n : rows * (n + 1)], o_hbm.at[rows * n : rows * (n + 1)], sem.at[n])
        for n in range(STORES)
    ]
    for copy in copies:
        copy.start()
    for copy in copies:
        copy.wait()


def store_call(y):
    return pl.pallas_call(
        store_kernel,
        in_specs=[pl.BlockSpec(memory_space=pltpu.VMEM)],
        out_specs=pl.BlockSpec(memory_space=pl.ANY),
        out_shape=jax.ShapeDtypeStruct(y.shape, y.dtype),
        scratch_shapes=[pltpu.SemaphoreType.DMA((STORES,))],
        compiler_params=pltpu.CompilerParams(vmem_limit_bytes=8 * 1024 * 1024),
        name="store",
    )(y)


def on_device(inputs, b_panel, c_panel, dt_raw, dt_bias, a_log, d_skip):
    y = layer_call(inputs, b_panel, c_panel, dt_raw, dt_bias[None], a_log[None], d_skip[None])
    return store_call(y)


def solution(mesh):
    return jax.shard_map(
        on_device,
        mesh=mesh,
        in_specs=(P(("seq", "head"), None),) * 4 + (P(), P(), P()),
        out_specs=P(("seq", "head"), None),
        check_vma=False,
    )
```

```python
import functools

import jax
import jax.numpy as jnp
from jax import lax
from jax.experimental import pallas as pl
from jax.experimental.pallas import tpu as pltpu
from jax.sharding import PartitionSpec as P

HEADS = 128
HDIM = 64
DSTATE = 128
TOK = 320
PIECES = HEADS // 2
PARTS = 4
TURNS = 4
XBLOCKS = 8
BATCH = 4
FILL = 24
MEET = 5
STORES = 4
LOG2E = 1.4426950408889634
F32 = jnp.float32
BF16 = jnp.bfloat16
VMEM_LIMIT = 56 * 1024 * 1024


def layer_kernel(cfg, x_hbm, b_hbm, c_hbm, dt_hbm, bias_hbm, alog_hbm, skip_hbm, o_ref,
                 b_ref, c_ref, dt_ref, bias_ref, alog_ref, skip_ref, skips,
                 x_ref, part_ref, fade_ref, a_ref, rt_ref, sm_ref, g_ref, bt_ref,
                 l_ref, fl, fr, fe, sl, sr, rs, rbuf, eb, za, pa, dec_own, dec_pre, dec_suf, rowdec,
                 in_sem, x_sem, fl_sem, fr_sem, fe_sem, left_sem, right_sem, rs_sem, rbuf_sem, eb_sem,
                 z_send, z_recv, p_send, p_recv):
    Z, Y, R, K, A, AO, B, C = cfg
    low = Z // 2 - 1
    seq = lax.axis_index("seq")
    head = lax.axis_index("head")
    y = head // Z
    z = head - y * Z
    r = seq * Y + y
    in_plane = (z == low) | (z == low + 1)
    groups = R // PARTS
    part = r // groups
    rest = lax.rem(r, groups)
    diagonal = groups % Y == 0
    group = rest // Y * Y + lax.rem(rest - part + PARTS * Y, Y) if diagonal else rest
    rows = DSTATE // PARTS

    def owner(g, p):
        return p * groups + (g // Y * Y + lax.rem(p + g, Y) if diagonal else g)

    def remote(src, dst, send, recv, to_seq, to_head):
        return pltpu.make_async_remote_copy(
            src_ref=src, dst_ref=dst, send_sem=send, recv_sem=recv,
            device_id={"seq": to_seq, "head": to_head}, device_id_type=pl.DeviceIdType.MESH,
        )

    def await_bytes(ref, sem):
        pltpu.make_async_copy(ref, ref, sem).wait()

    def send_left(src, q):
        remote(src, fr.at[q], left_sem, fr_sem.at[q], seq, head - 1).start()

    def send_right(src, q):
        remote(src, fl.at[q], right_sem, fl_sem.at[q], seq, head + 1).start()

    pairs = ((b_hbm, b_ref), (c_hbm, c_ref), (dt_hbm, dt_ref), (bias_hbm, bias_ref), (alog_hbm, alog_ref), (skip_hbm, skip_ref))
    loads = [pltpu.make_async_copy(src, dst, in_sem.at[n]) for n, (src, dst) in enumerate(pairs)]
    for copy in loads:
        copy.start()

    gate = pltpu.get_barrier_semaphore()

    def greet(to_seq, to_head):
        pl.semaphore_signal(
            gate, inc=1, device_id={"seq": to_seq, "head": to_head}, device_id_type=pl.DeviceIdType.MESH
        )

    for dz in range(1, Z):
        greet(seq, y * Z + lax.rem(z + dz, Z))

    @pl.when(in_plane)
    def _():
        def hello(d, carry):
            to = lax.rem(r + d, R)
            to_seq = to // Y
            greet(to_seq, (to - to_seq * Y) * Z + z)
            return carry

        lax.fori_loop(1, R, hello, 0)

    blocks = XBLOCKS
    width = K * 128 // blocks

    def x_copy(n):
        cols = pl.ds(pl.multiple_of(n * width, width), width)
        return pltpu.make_async_copy(x_hbm.at[:, cols], x_ref.at[:, cols], x_sem.at[n])

    for n in range(blocks):
        x_copy(n).start()

    for copy in loads:
        copy.wait()

    v = dt_ref[...].astype(F32) + bias_ref[...]
    delta = jnp.maximum(v, 0.0) + jnp.log(1.0 + jnp.exp(-jnp.abs(v)))
    rates = (-LOG2E) * jnp.exp(alog_ref[...]) * delta
    t_at = lax.broadcasted_iota(jnp.int32, (TOK, TOK), 0)
    s_at = lax.broadcasted_iota(jnp.int32, (TOK, TOK), 1)
    lower = (t_at >= s_at).astype(BF16)
    high = rates.astype(BF16)
    rest_1 = rates - high.astype(F32)
    mid = rest_1.astype(BF16)
    fine = (rest_1 - mid.astype(F32)).astype(BF16)
    sums = jnp.dot(lower, jnp.concatenate([high, mid, fine], axis=1), preferred_element_type=F32)
    a = sums[:, :HEADS] + (sums[:, HEADS : 2 * HEADS] + sums[:, 2 * HEADS :])
    a_ref[...] = a
    g_ref[...] = (jnp.exp2(a[TOK - 1 : TOK, :] - a) * delta).astype(BF16)
    bt_ref[...] = b_ref[...].astype(F32).T.astype(BF16)

    piece_at = lax.broadcasted_iota(jnp.int32, (K, 128), 0)
    head_at = lax.broadcasted_iota(jnp.int32, (K, 128), 1)
    pick_head = lax.broadcasted_iota(jnp.int32, (128, 128), 0)
    pick_lane = lax.broadcasted_iota(jnp.int32, (128, 128), 1) // HDIM

    def per_piece(value):
        second = (lax.rem(pick_head, 2) == pick_lane).astype(F32)
        only = jnp.where(head_at // 2 == piece_at, value, 0.0)
        logs = jnp.dot(only, second, precision=lax.Precision.HIGHEST, preferred_element_type=F32)
        return logs

    dec_own[...] = jnp.exp2(per_piece(a[TOK - 1 : TOK, :]))
    my_row = pl.ds(pl.multiple_of(z * 8, 8), 8)
    za[my_row, :] = jnp.broadcast_to(a[TOK - 1 : TOK, :], (8, 128))

    pl.semaphore_wait(gate, Z - 1 + jnp.where(in_plane, R - 1, 0))

    for dz in range(1, Z):
        remote(za.at[my_row, :], za.at[my_row, :], z_send, z_recv, seq, y * Z + lax.rem(z + dz, Z)).start()

    def meet_row():
        await_bytes(za.at[0 : 8 * (Z - 1), :], z_recv)
        before = jnp.zeros((8, 128), F32)
        after = jnp.zeros((8, 128), F32)
        for other in range(Z):
            value = za[8 * other : 8 * other + 8, :]
            before = before + jnp.where(other < z, value, 0.0)
            after = after + jnp.where(other > z, value, 0.0)
        total = before + after + za[my_row, :]

        @pl.when(in_plane)
        def _():
            slot = pl.ds(pl.multiple_of(r * 8, 8), 8)
            pa[slot, :] = total

            def tell(d, carry):
                to = lax.rem(r + d, R)
                to_seq = to // Y
                remote(
                    pa.at[slot, :], pa.at[slot, :], p_send, p_recv, to_seq, (to - to_seq * Y) * Z + z
                ).start()
                return carry

            lax.fori_loop(1, R, tell, 0)

        dec_pre[...] = jnp.exp2(per_piece(before[0:1, :]))
        dec_suf[...] = jnp.exp2(per_piece(after[0:1, :]))

    def score_tables():
        v = dt_ref[...].astype(F32) + bias_ref[...]
        delta = jnp.maximum(v, 0.0) + jnp.log(1.0 + jnp.exp(-jnp.abs(v)))
        rt_ref[...] = (a_ref[...] - jnp.log2(delta)).T
        scores = lax.dot_general(c_ref[...], b_ref[...], (((1,), (1,)), ((), ())), preferred_element_type=F32)
        t_at = lax.broadcasted_iota(jnp.int32, (TOK, TOK), 0)
        s_at = lax.broadcasted_iota(jnp.int32, (TOK, TOK), 1)
        sm_ref[...] = jnp.where(t_at >= s_at, scores, 0.0)
        skips[...] = per_piece(skip_ref[...])

    lane = lax.broadcasted_iota(jnp.int32, (TOK, 128), 1)
    first = lane < HDIM

    def columns_of(q):
        return pl.ds(pl.multiple_of(q * 128, 128), 128)

    wide_head = lax.broadcasted_iota(jnp.int32, (128, 128 * BATCH), 0)
    wide_lane = lax.broadcasted_iota(jnp.int32, (128, 128 * BATCH), 1) // HDIM

    def local_states(q):
        cols = pl.ds(pl.multiple_of(q * 128, 128 * BATCH), 128 * BATCH)
        spread = (wide_head == 2 * q + wide_lane).astype(BF16)
        gain = jnp.dot(g_ref[...], spread, preferred_element_type=F32)
        scaled = (x_ref[:, cols].astype(F32) * gain).astype(BF16)
        state = jnp.dot(bt_ref[...], scaled, preferred_element_type=F32).astype(BF16)
        for u in range(BATCH):
            l_ref[q + u] = state[:, 128 * u : 128 * (u + 1)]

    def within_and_skip(start):
        turned = pltpu.roll(a_ref[...], lax.rem(HEADS - 2 * start, HEADS), 1)
        for u in range(2):
            q = start + u
            x = x_ref[:, columns_of(q)]
            columns, parts = [], []
            for k in range(2):
                h = 2 * u + k
                column = jnp.broadcast_to(turned[:, h : h + 1], (TOK, 128))
                columns.append(column)
                row = rt_ref[pl.ds(2 * q + k, 1), :]
                outs = []
                for t0, t1 in ((0, 128), (128, 256), (256, TOK)):
                    tiles = []
                    for s0 in range(0, t1, 128):
                        s1 = min(s0 + 128, t1)
                        gap = column[t0:t1, : s1 - s0] - row[:, s0:s1]
                        if s1 > t0:
                            gap = jnp.minimum(gap, 100.0)
                        tiles.append((sm_ref[t0:t1, s0:s1] * jnp.exp2(gap)).astype(BF16))
                    w = jnp.concatenate(tiles, axis=1) if len(tiles) > 1 else tiles[0]
                    outs.append(jnp.dot(w, x[:t1], preferred_element_type=F32))
                parts.append(jnp.concatenate(outs, axis=0))
            fade_ref[q] = jnp.exp2(jnp.where(first, columns[0], columns[1]))
            part_ref[q] = jnp.where(first, parts[0], parts[1]) + skips[pl.ds(q, 1), :] * x.astype(F32)

    def finish(start):
        both = jnp.concatenate([fl[start], fl[start + 1]], axis=1)
        carried = jnp.dot(c_ref[...], both, preferred_element_type=F32)
        for u in range(2):
            q = start + u
            here = part_ref[q] + fade_ref[q] * carried[:, 128 * u : 128 * (u + 1)]
            o_ref[:, columns_of(q)] = here.astype(BF16)

    def tick(i, carry):
        @pl.when(i == MEET)
        def _():
            meet_row()

        for par in range(2):
            m = low + par
            q = i - (4 * A + B + C) - AO * jnp.abs(z - m)
            at = jnp.clip(q, 0, K - 1)
            k = at // 2
            valid = (q >= 0) & (q < K) & (lax.rem(at, 2) == par)

            @pl.when(valid & (z < m))
            def _():
                remote(sl.at[at], fr.at[at], left_sem, fr_sem.at[at], seq, head + 1).wait_recv()

                @pl.when(z > 0)
                def _():
                    send_left(fr.at[at], at)
                    fl[at] = (fl[at].astype(F32) + dec_pre[pl.ds(at, 1), :] * fr[at].astype(F32)).astype(BF16)

                @pl.when(z == 0)
                def _():
                    fl[at] = fr[at]

            @pl.when(valid & (z == m))
            def _():
                mine = group == lax.rem(k, groups)

                @pl.when(mine)
                def _():
                    await_bytes(fe.at[k, 0 : rows * (PARTS - 1)], fe_sem.at[k])

                @pl.when(jnp.logical_not(mine))
                def _():
                    await_bytes(fe.at[k], fe_sem.at[k])

                send_left(fe.at[k], at)
                entering = fl[at].astype(F32) + dec_pre[pl.ds(at, 1), :] * fe[k].astype(F32)
                fl[at] = entering.astype(BF16)
                sr[at] = (dec_own[pl.ds(at, 1), :] * entering + l_ref[at].astype(F32)).astype(BF16)
                send_right(sr.at[at], at)

            @pl.when(valid & (z > m))
            def _():
                remote(sr.at[at], fl.at[at], right_sem, fl_sem.at[at], seq, head - 1).wait_recv()

                @pl.when(z < Z - 1)
                def _():
                    sr[at] = (dec_own[pl.ds(at, 1), :] * fl[at].astype(F32) + l_ref[at].astype(F32)).astype(BF16)
                    send_right(sr.at[at], at)

        ahead = jnp.minimum(i, K - 1)
        per_block = K // XBLOCKS

        @pl.when((i < K) & (lax.rem(ahead, per_block) == 0))
        def _():
            x_copy(ahead // per_block).wait()

        @pl.when((i < K) & (lax.rem(ahead, BATCH) == 0))
        def _():
            local_states(pl.multiple_of(ahead, BATCH))

        q = i - A * z
        at = jnp.clip(q, 0, K - 1)
        valid = (q >= 0) & (q < K) & (z < low + lax.rem(at, 2))

        @pl.when(valid & (z == 0))
        def _():
            send_right(l_ref.at[at], at)

        @pl.when(valid & (z > 0))
        def _():
            remote(sr.at[at], fl.at[at], right_sem, fl_sem.at[at], seq, head - 1).wait_recv()
            sr[at] = (dec_own[pl.ds(at, 1), :] * fl[at].astype(F32) + l_ref[at].astype(F32)).astype(BF16)
            send_right(sr.at[at], at)

        q1 = i - A * (Z - 1 - z)
        at1 = jnp.clip(q1, 0, K - 1)
        valid1 = (q1 >= 0) & (q1 < K) & (z > low + lax.rem(at1, 2))

        @pl.when(valid1 & (z == Z - 1))
        def _():
            send_left(l_ref.at[at1], at1)

        @pl.when(valid1 & (z < Z - 1))
        def _():
            remote(sl.at[at1], fr.at[at1], left_sem, fr_sem.at[at1], seq, head + 1).wait_recv()
            sl[at1] = (dec_suf[pl.ds(at1, 1), :] * l_ref[at1].astype(F32) + fr[at1].astype(F32)).astype(BF16)
            send_left(sl.at[at1], at1)

        q2 = i - 4 * A
        at2 = jnp.clip(q2, 0, K - 1)
        k2 = at2 // 2

        @pl.when((q2 >= 0) & (q2 < K) & (z == low + lax.rem(at2, 2)))
        def _():
            remote(sr.at[at2], fl.at[at2], right_sem, fl_sem.at[at2], seq, head - 1).wait_recv()
            remote(sl.at[at2], fr.at[at2], left_sem, fr_sem.at[at2], seq, head + 1).wait_recv()
            inner = dec_own[pl.ds(at2, 1), :] * fl[at2].astype(F32) + l_ref[at2].astype(F32)
            total = (dec_suf[pl.ds(at2, 1), :] * inner + fr[at2].astype(F32)).astype(BF16)

            rs[k2] = total
            turn = k2 // groups
            for p in range(PARTS):
                to = owner(lax.rem(k2, groups), p)

                @pl.when(to == r)
                def _():
                    rbuf[turn, r] = total[rows * p : rows * (p + 1)]

                @pl.when(to != r)
                def _():
                    to_seq = to // Y
                    remote(
                        rs.at[k2, rows * p : rows * (p + 1)], rbuf.at[turn, r], rs_sem, rbuf_sem.at[turn],
                        to_seq, (to - to_seq * Y) * Z + z,
                    ).start()

        @pl.when(in_plane & (i == 4 * A))
        def _():
            await_bytes(pa.at[0 : 8 * (R - 1), :], p_recv)

        for turn in range(TURNS):
            k3 = group + turn * groups
            q3 = 2 * k3 + (z - low)

            @pl.when(in_plane & (i == q3 + 4 * A + B))
            def _():
                chosen = (pick_head == 2 * q3 + pick_lane).astype(F32)
                rowdec[...] = jnp.exp2(
                    jnp.dot(pa[...], chosen, precision=lax.Precision.HIGHEST, preferred_element_type=F32)
                )
                await_bytes(rbuf.at[turn, 0 : R - 1], rbuf_sem.at[turn])
                span = pl.ds(pl.multiple_of(part * rows, rows), rows)

                def row(s, run):
                    e = run.astype(BF16)

                    @pl.when(s == r)
                    def _():
                        fe[k3, span] = e

                    @pl.when(s != r)
                    def _():
                        eb[turn, s] = e
                        to_seq = s // Y
                        remote(
                            eb.at[turn, s], fe.at[k3, span], eb_sem, fe_sem.at[k3],
                            to_seq, (s - to_seq * Y) * Z + z,
                        ).start()

                    return rowdec[pl.ds(s * 8, 1), :] * run + rbuf[turn, s].astype(F32)

                lax.fori_loop(0, R, row, jnp.zeros((rows, 128), F32))

        @pl.when(i == 0)
        def _():
            score_tables()

        early = FILL // 2
        w = jnp.where(i < FILL, i // 2, early + (i - FILL) // 4)
        now = jnp.where(i < FILL, lax.rem(i, 2) == 0, lax.rem(i, 4) == 0)
        w_at = jnp.minimum(w, K // 2 - 1)

        @pl.when(now & (w < K // 2))
        def _():
            within_and_skip(2 * w_at)

        far = jnp.maximum(jnp.abs(z - low), jnp.abs(z - low - 1))
        done = i - (4 * A + B + C) - AO * far - 1
        done_at = jnp.clip(done, 0, K - 2)

        @pl.when((done >= 0) & (done < K - 1) & (lax.rem(done_at, 2) == 0))
        def _():
            finish(done_at)

        return carry

    lax.fori_loop(0, K + 4 * A + B + C + AO * (Z // 2), tick, 0)

    await_bytes(za.at[0 : 8 * (Z - 1), :], z_send)

    @pl.when(z > 0)
    def _():
        await_bytes(sl, left_sem)

    @pl.when(z < Z - 1)
    def _():
        await_bytes(sr, right_sem)

    @pl.when(in_plane)
    def _():
        await_bytes(pa.at[0 : 8 * (R - 1), :], p_send)
        for turn in range(TURNS):
            await_bytes(rbuf.at[turn, 0 : R - 1], rs_sem)
            await_bytes(rbuf.at[turn, 0 : R - 1], eb_sem)


def layer_call(x, b, c, dt, bias, alog, skip, Z=8, K=PIECES, A=6, AO=6, B=7, C=8):
    Y = lax.axis_size("head") // Z
    R = lax.axis_size("seq") * Y
    tile = (DSTATE, 128)
    dma = pltpu.SemaphoreType.DMA
    vmem = pl.BlockSpec(memory_space=pltpu.VMEM)
    hbm = pl.BlockSpec(memory_space=pl.ANY)
    small = pltpu.VMEM((R * 8, 128), F32)
    share = pltpu.VMEM((TURNS, R, DSTATE // PARTS, 128), BF16)
    return pl.pallas_call(
        functools.partial(layer_kernel, (Z, Y, R, K, A, AO, B, C)),
        in_specs=[hbm] * 7,
        out_specs=vmem,
        out_shape=pltpu.VMEM((TOK, K * 128), BF16) if K == PIECES else jax.ShapeDtypeStruct((TOK, K * 128), BF16),
        scratch_shapes=[
            pltpu.VMEM((TOK, DSTATE), BF16),
            pltpu.VMEM((TOK, DSTATE), BF16),
            pltpu.VMEM((TOK, HEADS), BF16),
            pltpu.VMEM((1, HEADS), F32),
            pltpu.VMEM((1, HEADS), F32),
            pltpu.VMEM((1, HEADS), F32),
            pltpu.VMEM((K, 128), F32),
            pltpu.VMEM((TOK, K * 128), BF16),
            pltpu.VMEM((K, TOK, 128), F32),
            pltpu.VMEM((K, TOK, 128), F32),
            pltpu.VMEM((TOK, HEADS), F32),
            pltpu.VMEM((HEADS, TOK), F32),
            pltpu.VMEM((TOK, TOK), F32),
            pltpu.VMEM((TOK, HEADS), BF16),
            pltpu.VMEM((DSTATE, TOK), BF16),
            pltpu.VMEM((K, *tile), BF16),
            pltpu.VMEM((K, *tile), BF16),
            pltpu.VMEM((K, *tile), BF16),
            pltpu.VMEM((K // 2, *tile), BF16),
            pltpu.VMEM((K, *tile), BF16),
            pltpu.VMEM((K, *tile), BF16),
            pltpu.VMEM((K // 2, *tile), BF16),
            share,
            share,
            pltpu.VMEM((Z * 8, 128), F32),
            small,
            pltpu.VMEM((K, 128), F32),
            pltpu.VMEM((K, 128), F32),
            pltpu.VMEM((K, 128), F32),
            small,
            dma((6,)), dma((XBLOCKS,)), dma((K,)), dma((K,)), dma((K // 2,)),
            dma, dma, dma, dma((TURNS,)), dma, dma, dma, dma, dma,
        ],
        compiler_params=pltpu.CompilerParams(
            vmem_limit_bytes=VMEM_LIMIT, has_side_effects=True, collective_id=0
        ),
        name="layer",
    )(x, b, c, dt, bias, alog, skip)


def store_kernel(y_ref, o_hbm, sem):
    rows = TOK // STORES
    copies = [
        pltpu.make_async_copy(y_ref.at[rows * n : rows * (n + 1)], o_hbm.at[rows * n : rows * (n + 1)], sem.at[n])
        for n in range(STORES)
    ]
    for copy in copies:
        copy.start()
    for copy in copies:
        copy.wait()


def store_call(y):
    return pl.pallas_call(
        store_kernel,
        in_specs=[pl.BlockSpec(memory_space=pltpu.VMEM)],
        out_specs=pl.BlockSpec(memory_space=pl.ANY),
        out_shape=jax.ShapeDtypeStruct(y.shape, y.dtype),
        scratch_shapes=[pltpu.SemaphoreType.DMA((STORES,))],
        compiler_params=pltpu.CompilerParams(vmem_limit_bytes=8 * 1024 * 1024),
        name="store",
    )(y)


def on_device(inputs, b_panel, c_panel, dt_raw, dt_bias, a_log, d_skip):
    y = layer_call(inputs, b_panel, c_panel, dt_raw, dt_bias[None], a_log[None], d_skip[None])
    return store_call(y)


def solution(mesh):
    return jax.shard_map(
        on_device,
        mesh=mesh,
        in_specs=(P(("seq", "head"), None),) * 4 + (P(), P(), P()),
        out_specs=P(("seq", "head"), None),
        check_vma=False,
    )
```
